512 devices in a mesh: nodes: 128 (over z, x, core), feat: 4 (over y).
Axes of the slice: x: 4, y: 4, z: 16, core: 2. Of those that a mesh axis runs over, the one named last changes fastest.
Arguments:
- x_t: bfloat16 [128, 16384], P('feat', 'nodes'), may hold values from -6 to 6
- weight: bfloat16 [128, 256], P('feat'), may hold values from -0.5 to 0.5
- block_cols: int32 [128, 16], P('nodes'), may hold values from 0 to 127, as said below
- block_count: int32 [128], P('nodes'), may hold values from 1 to 16, as said below
- block_vals: bfloat16 [128, 16, 128, 128], P('nodes'), may hold values from -0.125 to 0.125
- d_out_t: bfloat16 [256, 16384], P('feat', 'nodes'), may hold values from -6 to 6
Outputs:
- out_t: bfloat16 [256, 16384], P('feat', 'nodes')
- grad_w: float32 [128, 256], P('feat')
- grad_x_t: float32 [128, 16384], P('feat', 'nodes')
The draws below stay inside these ranges and needn't reach their ends.
Inputs may be any that keep to these rules, and one draw needn't show every extreme that they name: `block_cols`: each row of node blocks names 16 different node blocks. `block_count`: node block 0 has all 16 blocks live.
All inputs are finite; a program needn't handle non-finite values.
Results may differ from the reference program's by a relative error of at most 0.0055.
Values may be sent and summed in bfloat16 or wider, within the bound.
No kernel may reach another device: no remote copies, remote signals or barrier semaphores. Data moves between devices by JAX's collectives and lax.ppermute only.
A program may use at most 64 MiB of HBM per device.

```python
import jax
import jax.numpy as jnp
from jax import lax

F_IN = 128
HID = 256
B = 128
K = 16
NB_DEV = 1
NBLK = 128
NODES = 16384
N_NODES = 128


def draw_block_cols(key, part):
    key = jax.random.fold_in(key, 5)
    key_sub, key_boost, key_noise = jax.random.split(key, 3)
    owner_range = jnp.arange(N_NODES, dtype=jnp.int32)
    sub_pick = jax.random.randint(key_sub, (N_NODES, N_NODES), 0, NB_DEV)
    sub_pick = sub_pick.at[:, 0].set(0).at[:, N_NODES - 1].set(NB_DEV - 1)
    boost = jax.random.randint(key_boost, (N_NODES,), 0, 4) * 16384
    boost = boost.at[0].set(131072).at[N_NODES - 1].set(131072)
    noise = jax.random.randint(key_noise, (NBLK, N_NODES), 0, 65536)
    score = (noise + boost[None, :]) * N_NODES + owner_range[None, :]
    _, owners = lax.top_k(score, K)
    device = jnp.arange(NBLK, dtype=jnp.int32) // NB_DEV
    chosen = sub_pick[device[:, None], owners]
    return (owners * NB_DEV + chosen).astype(jnp.int32)


def draw_block_count(key, part):
    key = jax.random.fold_in(key, 11)
    counts = jax.random.randint(key, (NBLK,), 1, K + 1)
    return counts.at[0].set(K).astype(jnp.int32)


def steps_of(rng, dims, shards, low, high):
    def one(axis_at, shards_of):
        heights = jax.random.uniform(jax.random.fold_in(jax.random.fold_in(rng, 6), axis_at), (shards_of,), jnp.float32, low / len(shards), high / len(shards))
        return jnp.repeat(jnp.exp(heights), dims[axis_at] // shards_of).reshape((-1,) + (1,) * (len(dims) - axis_at - 1))

    loudness = one(*shards[0])
    for cut in shards[1:]:
        loudness = loudness * one(*cut)
    return loudness


def bell_draw(rng, dims, deviation, limit, pieces=(), held_as=jnp.bfloat16):
    drawn = jax.random.normal(rng, dims, jnp.float32) * deviation
    if len(pieces) > 0:
        drawn = steps_of(rng, dims, pieces, -0.22, 0.18) * drawn
    return jnp.clip(drawn, min=-limit, max=limit).astype(held_as)


def setup_inputs(seed: int = 0) -> dict:
    splits = jax.random.split(jax.random.key(seed), 7)
    return {
        "x_t": bell_draw(splits[0], (F_IN, NODES), 1.0, 6.0, ((0, 4), (1, 128))),
        "weight": bell_draw(splits[1], (F_IN, HID), F_IN ** -0.5, 0.5, ((0, 4),)),
        "block_cols": draw_block_cols(jax.random.fold_in(splits[6], 71), 0),
        "block_count": draw_block_count(jax.random.fold_in(splits[6], 71), 0),
        "block_vals": bell_draw(splits[4], (NBLK, K, B, B), (B * K) ** -0.5, 0.125, ((0, 128),)),
        "d_out_t": bell_draw(splits[5], (HID, NODES), 1.0, 6.0, ((0, 4), (1, 128))),
    }


def gelu_fn(value):
    return jax.nn.gelu(value, approximate=True)

def reference(x_t, weight, block_cols, block_count, block_vals, d_out_t):
    live = (jnp.arange(K)[None, :] < block_count[:, None]).astype(jnp.float32)
    x_blocks = x_t.reshape(F_IN, NBLK, B)

    def one_row(items):
        cols, keep, vals = items
        picked = x_blocks[:, cols, :].astype(jnp.float32)
        masked = vals.astype(jnp.float32) * keep[:, None, None]
        return jnp.einsum('fkj,kij->fi', picked, masked)
    agg = lax.map(one_row, (block_cols, live, block_vals))
    agg_t = jnp.transpose(agg, (1, 0, 2)).reshape(F_IN, NODES).astype(jnp.bfloat16)
    pre_t = jnp.dot(weight.T, agg_t, preferred_element_type=jnp.float32)
    out_t = gelu_fn(pre_t).astype(jnp.bfloat16)
    _, pull = jax.vjp(gelu_fn, pre_t)
    grad_pre_t = pull(d_out_t.astype(jnp.float32))[0].astype(jnp.bfloat16)
    grad_w = jnp.dot(agg_t, grad_pre_t.T, preferred_element_type=jnp.float32)
    grad_agg_t = jnp.dot(weight, grad_pre_t, preferred_element_type=jnp.float32).astype(jnp.bfloat16)
    grad_rowwise = jnp.transpose(grad_agg_t.reshape(F_IN, NBLK, B), (1, 0, 2))

    def add_row(total, items):
        cols, keep, vals, grad_row = items
        masked = vals.astype(jnp.float32) * keep[:, None, None]
        contrib = jnp.einsum('fi,kij->fkj', grad_row.astype(jnp.float32), masked)
        return (total.at[:, cols, :].add(contrib), None)
    start = jnp.zeros((F_IN, NBLK, B), jnp.float32)
    total, _ = lax.scan(add_row, start, (block_cols, live, block_vals, grad_rowwise))
    grad_x_t = total.reshape(F_IN, NODES)
    return (out_t, grad_w, grad_x_t)
```

```python
import jax
import jax.numpy as jnp
from jax import lax
from jax.experimental import pallas as pl
from jax.experimental.pallas import tpu as pltpu
from jax.sharding import Mesh, PartitionSpec as P

BF = jnp.bfloat16
F32 = jnp.float32
NZ, NX, NC, NY = 16, 4, 2, 4
K, B, FL, HL = 16, 128, 32, 64
QK = K // NY
D_AT, W_AT = QK * B, QK * B + HL
ROWS = W_AT + 2 * FL
PACK = FL + 2 * B + FL
C0, C1 = 0.7978845608, 0.044715
VM = pltpu.CompilerParams(vmem_limit_bytes=32 * 1024 * 1024)
VMEM = pl.BlockSpec(memory_space=pltpu.VMEM)
SMEM = pl.BlockSpec(memory_space=pltpu.SMEM)


def dot(a, b, ca, cb):
    return lax.dot_general(a, b, (((ca,), (cb,)), ((), ())), preferred_element_type=F32)


def agg_kernel(idx, ids, xg, g, out):
    core = ids[0]
    for r in range(NC):
        acc = jnp.zeros((FL, B), F32)
        for s in range(K):
            owner = idx[r, s]
            use = jnp.logical_and(owner % NC == core, s < idx[r, K])
            got = xg[(owner // NC) % NX, owner // (NC * NX)]
            got = jnp.where(use, got, jnp.zeros_like(got))
            vals = g[r * NY + s // QK, (s % QK) * B : (s % QK + 1) * B, :]
            acc = acc + dot(got, vals, 1, 1)
        for y in range(NY):
            out[r * NY + y] = acc


def mid_kernel(ids, parts, g, out_t, pack):
    core, y_at = ids[0], ids[1]
    agg = [(parts[y] + parts[NY + y]).astype(BF) for y in range(NY)]
    agg_all = jnp.concatenate(agg, axis=0)
    for h in range(2):
        w = jnp.concatenate(
            [g[y, W_AT + h * FL : W_AT + (h + 1) * FL, :] for y in range(NY)], axis=0
        )
        pre = dot(w, agg_all, 0, 0)
        t = jnp.tanh(C0 * (pre + C1 * (pre * pre * pre)))
        val = (0.5 * pre * (1.0 + t)).astype(BF)
        der = 0.5 * (1.0 + t) + 0.5 * pre * (1.0 - t * t) * (C0 * (1.0 + 3.0 * C1 * (pre * pre)))
        for q in range(2):
            y = 2 * h + q

            @pl.when(y_at == y)
            def _():
                out_t[...] = val[q * HL : (q + 1) * HL]

            cot = g[core * NY + y, D_AT : D_AT + HL, :].astype(F32)
            at = FL + y * HL
            pack[at : at + HL, :] = (cot * der[q * HL : (q + 1) * HL]).astype(BF)
    own = sum(jnp.where(y_at == y, (parts[y] + parts[NY + y]), 0.0) for y in range(NY))
    pack[0:FL, :] = own.astype(BF)
    back = jnp.zeros((FL, B), F32)
    for h in range(2):
        w_own = g[y_at, W_AT + h * FL : W_AT + (h + 1) * FL, :]
        back = back + dot(w_own, pack[FL + h * B : FL + (h + 1) * B, :], 1, 0)
    pack[FL + 2 * B : PACK, :] = back.astype(BF)


def back_kernel(idx, ids, both, g, out, term):
    core = ids[0]
    term[...] = jnp.zeros_like(term)
    gw = jnp.zeros((FL, B), F32)
    for r in range(NC):
        half = both[r, pl.ds(pl.multiple_of(FL + core * B, FL), B), :]
        gw = gw + dot(both[r, 0:FL, :], half, 1, 1)
        grad = both[r, FL + 2 * B : PACK, :]
        for s in range(K):
            owner = idx[r, s]
            use = jnp.logical_and(owner % NC == core, s < idx[r, K])
            at = ((owner // NC) % NX) * NZ + owner // (NC * NX)
            at = jnp.where(use, at, NX * NZ)
            vals = g[r * NY + s // QK, (s % QK) * B : (s % QK + 1) * B, :]
            term[at] = term[at] + dot(grad, vals, 1, 0)
    gw = gw.astype(BF)
    for x in range(NX):
        for z in range(NZ):
            out[x, z * FL : (z + 1) * FL, :] = term[x * NZ + z].astype(BF)
        out[x, NZ * FL :, :] = gw


def sum_kernel(got, out):
    gw = sum(got[x, NZ * FL :, :].astype(F32) for x in range(NX)).astype(BF)
    for z in range(NZ):
        rows = slice(z * FL, (z + 1) * FL)
        out[z, 0:FL, :] = sum(got[x, rows, :].astype(F32) for x in range(NX)).astype(BF)
        out[z, FL:, :] = gw


def local(x_t, weight, block_cols, block_count, block_vals, d_out_t):
    core, y_at = lax.axis_index("c"), lax.axis_index("y")
    ids = jnp.stack([core, y_at]).astype(jnp.int32)
    with jax.named_scope("gather_small"):
        idx = jnp.concatenate([block_cols, block_count[:, None]], axis=1)
        idx = lax.all_gather(idx, "c", axis=0, tiled=True)
    with jax.named_scope("gather_vals"):
        quarter = lax.dynamic_slice_in_dim(
            block_vals.reshape(K * B, B), y_at * (QK * B), QK * B, axis=0
        )
        mine = jnp.concatenate([quarter, d_out_t, weight[:, :B], weight[:, B:]], axis=0)
        g = lax.all_gather(mine, ("c", "y"), axis=0, tiled=False)
    with jax.named_scope("gather_x"):
        a = lax.all_to_all(jnp.broadcast_to(x_t, (NZ, FL, B)), "z", 0, 0, tiled=True)
        a = lax.all_to_all(jnp.broadcast_to(a, (NX, NZ, FL, B)), "x", 0, 0, tiled=True)
    parts = pl.pallas_call(
        agg_kernel,
        out_shape=jax.ShapeDtypeStruct((NC * NY, FL, B), F32),
        in_specs=[SMEM, SMEM, VMEM, VMEM],
        out_specs=VMEM,
        compiler_params=VM,
        name="agg",
    )(idx, ids, a, g)
    with jax.named_scope("share_agg"):
        parts = lax.all_to_all(parts, ("c", "y"), 0, 0, tiled=True)
    out_t, pack = pl.pallas_call(
        mid_kernel,
        out_shape=(
            jax.ShapeDtypeStruct((HL, B), BF),
            jax.ShapeDtypeStruct((PACK, B), BF),
        ),
        in_specs=[SMEM, VMEM, VMEM],
        out_specs=(VMEM, VMEM),
        compiler_params=VM,
        name="mid",
    )(ids, parts, g)
    with jax.named_scope("share_pair"):
        both = lax.all_gather(pack, "c", axis=0, tiled=False)
    term = pl.pallas_call(
        back_kernel,
        out_shape=jax.ShapeDtypeStruct((NX, NZ * FL + FL, B), BF),
        in_specs=[SMEM, SMEM, VMEM, VMEM],
        out_specs=VMEM,
        scratch_shapes=[pltpu.VMEM((NX * NZ + 1, FL, B), F32)],
        compiler_params=VM,
        name="back",
    )(idx, ids, both, g)
    with jax.named_scope("scatter_x"):
        term = lax.all_to_all(term, "x", 0, 0, tiled=True)
    term = pl.pallas_call(
        sum_kernel,
        out_shape=jax.ShapeDtypeStruct((NZ, 2 * FL, B), BF),
        in_specs=[VMEM],
        out_specs=VMEM,
        compiler_params=VM,
        name="sum_x",
    )(term)
    with jax.named_scope("scatter_z"):
        term = lax.all_to_all(term, "z", 0, 0, tiled=True)
        total = jnp.sum(term.astype(F32), axis=0)
    with jax.named_scope("join_w"):
        grad_w = lax.all_gather(total[FL:], "c", axis=1, tiled=True)
    return (out_t, grad_w, total[:FL])


def solution(mesh):
    fine = Mesh(mesh.devices.reshape(NZ, NX, NC, NY), ("z", "x", "c", "y"))
    nodes = ("z", "x", "c")
    return jax.shard_map(
        local,
        mesh=fine,
        in_specs=(
            P("y", nodes),
            P("y", None),
            P(nodes, None),
            P(nodes),
            P(nodes, None, None, None),
            P("y", nodes),
        ),
        out_specs=(P("y", nodes), P("y", None), P("y", nodes)),
        check_vma=False,
    )
```

```python
import jax
import jax.numpy as jnp
from jax import lax
from jax.experimental import pallas as pl
from jax.experimental.pallas import tpu as pltpu
from jax.sharding import Mesh, PartitionSpec as P

BF = jnp.bfloat16
F32 = jnp.float32
NZ, NX, NC, NY = 16, 4, 2, 4
K, B, FL, HL = 16, 128, 32, 64
META = K * B
ROWS = META + 16
RIDE = FL + HL + 2 * FL
PACK = FL + 2 * B + FL
C0, C1 = 0.7978845608, 0.044715
VM = pltpu.CompilerParams(vmem_limit_bytes=32 * 1024 * 1024)
VMEM = pl.BlockSpec(memory_space=pltpu.VMEM)
SMEM = pl.BlockSpec(memory_space=pltpu.SMEM)
HBM = pl.BlockSpec(memory_space=pl.ANY)


def dot(a, b, ca, cb):
    return lax.dot_general(a, b, (((ca,), (cb,)), ((), ())), preferred_element_type=F32)


def call(kernel, outs, name, ins, scratch=()):
    specs, args = zip(*ins)
    one = not isinstance(outs, list)
    shapes = [jax.ShapeDtypeStruct(*o) for o in ((outs,) if one else outs)]
    return pl.pallas_call(
        kernel,
        out_shape=shapes[0] if one else tuple(shapes),
        in_specs=list(specs),
        out_specs=VMEM if one else tuple(VMEM for _ in shapes),
        scratch_shapes=list(scratch),
        compiler_params=VM,
        name=name,
    )(*args)


def prep_kernel(cols, count, x, vals, mine, xb, sem):
    copy = pltpu.make_async_copy(vals, mine.at[0:META], sem)
    copy.start()
    for z in range(NZ):
        xb[z] = x[...]
    lane = lax.broadcasted_iota(jnp.int32, (16, B), 1)
    meta = jnp.where(lane == K, count[0], 0)
    for s in range(K):
        meta = jnp.where(lane == s, cols[0, s], meta)
    mine[META:ROWS, :] = meta.astype(F32).astype(BF)
    copy.wait()


def agg_kernel(mine, peer, xg, out, idx, ints, sem):
    core = lax.axis_index("c")
    idx[0] = mine[META:ROWS, :].astype(F32)[0:8].astype(jnp.int32)
    idx[1] = peer[META:ROWS, :].astype(F32)[0:8].astype(jnp.int32)
    copy = pltpu.make_async_copy(idx, ints, sem)
    copy.start()
    copy.wait()
    for r, blocks in enumerate((mine, peer)):
        acc = jnp.zeros((FL, B), F32)
        for s in range(K):
            owner = ints[r, 0, s]
            use = jnp.logical_and(owner % NC == core, s < ints[r, 0, K])
            got = xg[(owner // NC) % NX, owner // (NC * NX)]
            got = jnp.where(use, got, jnp.zeros_like(got))
            acc = acc + dot(got, blocks[s * B : (s + 1) * B, :], 1, 1)
        out[r] = acc


def ride_kernel(parts, d_out, weight, out):
    core = lax.axis_index("c")
    agg = (parts[core, 0] + parts[1 - core, 1]).astype(BF)
    for y in range(NY):
        out[y, 0:FL, :] = agg
        out[y, FL : FL + HL, :] = d_out[...]
        out[y, FL + HL : 2 * FL + HL, :] = weight[:, :B]
        out[y, 2 * FL + HL :, :] = weight[:, B:]


def mid_kernel(got, out_t, pack):
    y_at = lax.axis_index("y")
    agg = jnp.concatenate([got[y, 0:FL, :] for y in range(NY)], axis=0)
    pack[0:FL, :] = got[y_at, 0:FL, :]
    back = jnp.zeros((FL, B), F32)
    for h in range(2):
        rows = slice(FL + HL + h * FL, FL + HL + (h + 1) * FL)
        w = jnp.concatenate([got[y, rows, :] for y in range(NY)], axis=0)
        pre = dot(w, agg, 0, 0)
        t = jnp.tanh(C0 * (pre + C1 * (pre * pre * pre)))
        val = (0.5 * pre * (1.0 + t)).astype(BF)
        der = 0.5 * (1.0 + t) + 0.5 * pre * (1.0 - t * t) * (C0 * (1.0 + 3.0 * C1 * (pre * pre)))
        for q in range(2):
            y = 2 * h + q

            @pl.when(y_at == y)
            def _():
                out_t[...] = val[q * HL : (q + 1) * HL]

        cot = jnp.concatenate([got[2 * h + q, FL : FL + HL, :] for q in range(2)], axis=0)
        grad = (cot.astype(F32) * der).astype(BF)
        pack[FL + h * B : FL + (h + 1) * B, :] = grad
        back = back + dot(got[y_at, rows, :], grad, 1, 0)
    pack[FL + 2 * B : PACK, :] = back.astype(BF)


def back_kernel(idx, both, mine, peer, out, term):
    core = lax.axis_index("c")
    term[...] = jnp.zeros_like(term)
    gw = jnp.zeros((FL, B), F32)
    for r, blocks in enumerate((mine, peer)):
        row = core if r == 0 else 1 - core
        half = both[row, pl.ds(pl.multiple_of(FL + core * B, FL), B), :]
        gw = gw + dot(both[row, 0:FL, :], half, 1, 1)
        grad = both[row, FL + 2 * B : PACK, :]
        for s in range(K):
            owner = idx[r, 0, s]
            use = jnp.logical_and(owner % NC == core, s < idx[r, 0, K])
            at = ((owner // NC) % NX) * NZ + owner // (NC * NX)
            at = jnp.where(use, at, NX * NZ)
            term[at] = term[at] + dot(grad, blocks[s * B : (s + 1) * B, :], 1, 0)
    gw = gw.astype(BF)
    for x in range(NX):
        for z in range(NZ):
            out[x, z * FL : (z + 1) * FL, :] = term[x * NZ + z].astype(BF)
        out[x, NZ * FL :, :] = gw


def sum_kernel(got, out):
    gw = sum(got[x, NZ * FL :, :].astype(F32) for x in range(NX)).astype(BF)
    for z in range(NZ):
        rows = slice(z * FL, (z + 1) * FL)
        out[z, 0:FL, :] = sum(got[x, rows, :].astype(F32) for x in range(NX)).astype(BF)
        out[z, FL:, :] = gw


def half_kernel(got, out):
    out[...] = sum(got[z, FL:, :].astype(F32) for z in range(NZ))


def last_kernel(got, halves, grad_w, grad_x):
    grad_w[:, :B] = halves[0]
    grad_w[:, B:] = halves[1]
    grad_x[...] = sum(got[z, 0:FL, :].astype(F32) for z in range(NZ))


def local(x_t, weight, block_cols, block_count, block_vals, d_out_t):
    mine, xb = call(
        prep_kernel,
        [((ROWS, B), BF), ((NZ, FL, B), BF)],
        "prep",
        [
            (SMEM, block_cols),
            (SMEM, block_count),
            (VMEM, x_t),
            (HBM, block_vals.reshape(K * B, B)),
        ],
        [pltpu.SemaphoreType.DMA],
    )
    with jax.named_scope("swap_vals"):
        peer = lax.ppermute(mine, "c", [(0, 1), (1, 0)])
    with jax.named_scope("gather_x"):
        a = lax.all_to_all(xb, "z", 0, 0, tiled=True)
        a = lax.all_to_all(jnp.broadcast_to(a, (NX, NZ, FL, B)), "x", 0, 0, tiled=True)
    parts, idx = call(
        agg_kernel,
        [((NC, FL, B), F32), ((NC, 8, B), jnp.int32)],
        "agg",
        [(VMEM, mine), (VMEM, peer), (VMEM, a)],
        [pltpu.SMEM((NC, 8, B), jnp.int32), pltpu.SemaphoreType.DMA],
    )
    with jax.named_scope("pair_agg"):
        parts = lax.all_gather(parts, "c", axis=0, tiled=False)
    ride = call(
        ride_kernel,
        ((NY, RIDE, B), BF),
        "ride",
        [(VMEM, parts), (VMEM, d_out_t), (VMEM, weight)],
    )
    with jax.named_scope("share_agg"):
        ride = lax.all_to_all(ride, "y", 0, 0, tiled=True)
    out_t, pack = call(mid_kernel, [((HL, B), BF), ((PACK, B), BF)], "mid", [(VMEM, ride)])
    with jax.named_scope("share_pair"):
        both = lax.all_gather(pack, "c", axis=0, tiled=False)
    term = call(
        back_kernel,
        ((NX, NZ * FL + FL, B), BF),
        "back",
        [(SMEM, idx), (VMEM, both), (VMEM, mine), (VMEM, peer)],
        [pltpu.VMEM((NX * NZ + 1, FL, B), F32)],
    )
    with jax.named_scope("scatter_x"):
        term = lax.all_to_all(term, "x", 0, 0, tiled=True)
    term = call(sum_kernel, ((NZ, 2 * FL, B), BF), "sum_x", [(VMEM, term)])
    with jax.named_scope("scatter_z"):
        term = lax.all_to_all(term, "z", 0, 0, tiled=True)
    half = call(half_kernel, ((FL, B), F32), "half", [(VMEM, term)])
    with jax.named_scope("join_w"):
        halves = lax.all_gather(half, "c", axis=0, tiled=False)
    grad_w, grad_x = call(
        last_kernel,
        [((FL, 2 * B), F32), ((FL, B), F32)],
        "last",
        [(VMEM, term), (VMEM, halves)],
    )
    return (out_t, grad_w, grad_x)


def solution(mesh):
    fine = Mesh(mesh.devices.reshape(NZ, NX, NC, NY), ("z", "x", "c", "y"))
    nodes = ("z", "x", "c")
    return jax.shard_map(
        local,
        mesh=fine,
        in_specs=(
            P("y", nodes),
            P("y", None),
            P(nodes, None),
            P(nodes),
            P(nodes, None, None, None),
            P("y", nodes),
        ),
        out_specs=(P("y", nodes), P("y", None), P("y", nodes)),
        check_vma=False,
    )
```

```python
import jax
import jax.numpy as jnp
from jax import lax
from jax.experimental import pallas as pl
from jax.experimental.pallas import tpu as pltpu
from jax.sharding import Mesh, PartitionSpec as P

BF = jnp.bfloat16
F32 = jnp.float32
NZ, NX, NC, NY = 16, 4, 2, 4
K, B, FL, HL = 16, 128, 32, 64
SMALL = HL + 16
RIDE = NC * FL + NC * HL + 2 * FL
D_AT, W_AT = NC * FL, NC * FL + NC * HL
C0, C1 = 0.7978845608, 0.044715
VM = pltpu.CompilerParams(vmem_limit_bytes=32 * 1024 * 1024)
VMEM = pl.BlockSpec(memory_space=pltpu.VMEM)
SMEM = pl.BlockSpec(memory_space=pltpu.SMEM)


def dot(a, b, ca, cb):
    return lax.dot_general(a, b, (((ca,), (cb,)), ((), ())), preferred_element_type=F32)


def call(kernel, outs, name, ins, scratch=()):
    specs, args = zip(*ins)
    one = not isinstance(outs, list)
    shapes = [jax.ShapeDtypeStruct(*o) for o in ((outs,) if one else outs)]
    return pl.pallas_call(
        kernel,
        out_shape=shapes[0] if one else tuple(shapes),
        in_specs=list(specs),
        out_specs=VMEM if one else tuple(VMEM for _ in shapes),
        scratch_shapes=list(scratch),
        compiler_params=VM,
        name=name,
    )(*args)


def small_kernel(cols, count, d_out, out):
    lane = lax.broadcasted_iota(jnp.int32, (16, B), 1)
    meta = jnp.where(lane == K, count[0], 0)
    for s in range(K):
        meta = jnp.where(lane == s, cols[0, s], meta)
    out[0:HL, :] = d_out[...]
    out[HL:, :] = meta.astype(F32).astype(BF)


def agg_kernel(small, other, mine, peer, xg, out, idx, ints, sem):
    core = lax.axis_index("c")
    for r, got in enumerate((small, other)):
        idx[r] = got[HL:, :].astype(F32)[0:8].astype(jnp.int32)
    copy = pltpu.make_async_copy(idx, ints, sem)
    copy.start()
    copy.wait()
    for r, blocks in enumerate((mine, peer)):
        acc = jnp.zeros((FL, B), F32)
        for s in range(K):
            owner = ints[r, 0, s]
            use = jnp.logical_and(owner % NC == core, s < ints[r, 0, K])
            got = xg[(owner // NC) % NX, owner // (NC * NX)]
            got = jnp.where(use, got, jnp.zeros_like(got))
            acc = acc + dot(got, blocks[s * B : (s + 1) * B, :], 1, 1)
        out[r] = acc


def ride_kernel(parts, small, other, weight, out):
    core = lax.axis_index("c")
    for y in range(NY):
        out[y, W_AT : W_AT + FL, :] = weight[:, :B]
        out[y, W_AT + FL :, :] = weight[:, B:]
    for c in range(NC):
        agg = (parts[c, 0] + parts[1 - c, 1]).astype(BF)
        cot = jnp.where(core == c, small[0:HL, :].astype(F32), other[0:HL, :].astype(F32))
        for y in range(NY):
            out[y, c * FL : (c + 1) * FL, :] = agg
            out[y, D_AT + c * HL : D_AT + (c + 1) * HL, :] = cot.astype(BF)


def back_kernel(idx, got, mine, peer, out_t, out, term, hidden):
    core, y_at = lax.axis_index("c"), lax.axis_index("y")
    term[...] = jnp.zeros_like(term)
    agg = jnp.concatenate(
        [
            jnp.concatenate([got[y, c * FL : (c + 1) * FL, :] for y in range(NY)], axis=0)
            for c in range(NC)
        ],
        axis=1,
    )
    own = jnp.concatenate([got[y_at, c * FL : (c + 1) * FL, :] for c in range(NC)], axis=1)
    back = jnp.zeros((FL, NC * B), F32)
    for h in range(2):
        rows = slice(W_AT + h * FL, W_AT + (h + 1) * FL)
        w = jnp.concatenate([got[y, rows, :] for y in range(NY)], axis=0)
        pre = dot(w, agg, 0, 0)
        t = jnp.tanh(C0 * (pre + C1 * (pre * pre * pre)))
        val = (0.5 * pre * (1.0 + t)).astype(BF)
        der = 0.5 * (1.0 + t) + 0.5 * pre * (1.0 - t * t) * (C0 * (1.0 + 3.0 * C1 * (pre * pre)))
        for c in range(NC):
            for q in range(2):

                @pl.when(jnp.logical_and(core == c, y_at == 2 * h + q))
                def _():
                    out_t[...] = val[q * HL : (q + 1) * HL, c * B : (c + 1) * B]

        cot = jnp.concatenate(
            [
                jnp.concatenate(
                    [got[2 * h + q, D_AT + c * HL : D_AT + (c + 1) * HL, :] for q in range(2)],
                    axis=0,
                )
                for c in range(NC)
            ],
            axis=1,
        )
        grad = (cot.astype(F32) * der).astype(BF)
        hidden[h] = grad
        back = back + dot(got[y_at, rows, :], grad, 1, 0)
    gw = dot(own, hidden[core], 1, 1).astype(BF)
    back = back.astype(BF)
    for r, blocks in enumerate((mine, peer)):
        mix = back[:, :B], back[:, B:]
        first = core == 0 if r == 0 else core == 1
        grad = jnp.where(first, mix[0], mix[1])
        for s in range(K):
            owner = idx[r, 0, s]
            use = jnp.logical_and(owner % NC == core, s < idx[r, 0, K])
            at = ((owner // NC) % NX) * NZ + owner // (NC * NX)
            at = jnp.where(use, at, NX * NZ)
            term[at] = term[at] + dot(grad, blocks[s * B : (s + 1) * B, :], 1, 0)
    for x in range(NX):
        for z in range(NZ):
            out[x, z * FL : (z + 1) * FL, :] = term[x * NZ + z].astype(BF)
        out[x, NZ * FL :, :] = gw


def sum_kernel(got, out):
    gw = sum(got[x, NZ * FL :, :].astype(F32) for x in range(NX)).astype(BF)
    for z in range(NZ):
        rows = slice(z * FL, (z + 1) * FL)
        out[z, 0:FL, :] = sum(got[x, rows, :].astype(F32) for x in range(NX)).astype(BF)
        out[z, FL:, :] = gw


def half_kernel(got, out):
    out[...] = sum(got[z, FL:, :].astype(F32) for z in range(NZ))


def last_kernel(got, halves, grad_w, grad_x):
    grad_w[:, :B] = halves[0]
    grad_w[:, B:] = halves[1]
    grad_x[...] = sum(got[z, 0:FL, :].astype(F32) for z in range(NZ))


def local(x_t, weight, block_cols, block_count, block_vals, d_out_t):
    mine = block_vals.reshape(K * B, B)
    with jax.named_scope("gather_x"):
        a = lax.all_to_all(jnp.broadcast_to(x_t, (NZ, FL, B)), "z", 0, 0, tiled=True)
    small = call(
        small_kernel,
        ((SMALL, B), BF),
        "small",
        [(SMEM, block_cols), (SMEM, block_count), (VMEM, d_out_t)],
    )
    with jax.named_scope("swap_core"):
        peer = lax.ppermute(mine, "c", [(0, 1), (1, 0)])
        other = lax.ppermute(small, "c", [(0, 1), (1, 0)])
    with jax.named_scope("gather_x"):
        a = lax.all_to_all(jnp.broadcast_to(a, (NX, NZ, FL, B)), "x", 0, 0, tiled=True)
    parts, idx = call(
        agg_kernel,
        [((NC, FL, B), F32), ((NC, 8, B), jnp.int32)],
        "agg",
        [(VMEM, small), (VMEM, other), (VMEM, mine), (VMEM, peer), (VMEM, a)],
        [pltpu.SMEM((NC, 8, B), jnp.int32), pltpu.SemaphoreType.DMA],
    )
    with jax.named_scope("pair_agg"):
        parts = lax.all_gather(parts, "c", axis=0, tiled=False)
    ride = call(
        ride_kernel,
        ((NY, RIDE, B), BF),
        "ride",
        [(VMEM, parts), (VMEM, small), (VMEM, other), (VMEM, weight)],
    )
    with jax.named_scope("share_agg"):
        ride = lax.all_to_all(ride, "y", 0, 0, tiled=True)
    out_t, term = call(
        back_kernel,
        [((HL, B), BF), ((NX, NZ * FL + FL, B), BF)],
        "back",
        [(SMEM, idx), (VMEM, ride), (VMEM, mine), (VMEM, peer)],
        [pltpu.VMEM((NX * NZ + 1, FL, B), F32), pltpu.VMEM((2, B, NC * B), BF)],
    )
    with jax.named_scope("scatter_x"):
        term = lax.all_to_all(term, "x", 0, 0, tiled=True)
    term = call(sum_kernel, ((NZ, 2 * FL, B), BF), "sum_x", [(VMEM, term)])
    with jax.named_scope("scatter_z"):
        term = lax.all_to_all(term, "z", 0, 0, tiled=True)
    half = call(half_kernel, ((FL, B), F32), "half", [(VMEM, term)])
    with jax.named_scope("join_w"):
        halves = lax.all_gather(half, "c", axis=0, tiled=False)
    grad_w, grad_x = call(
        last_kernel,
        [((FL, 2 * B), F32), ((FL, B), F32)],
        "last",
        [(VMEM, term), (VMEM, halves)],
    )
    return (out_t, grad_w, grad_x)


def solution(mesh):
    fine = Mesh(mesh.devices.reshape(NZ, NX, NC, NY), ("z", "x", "c", "y"))
    nodes = ("z", "x", "c")
    return jax.shard_map(
        local,
        mesh=fine,
        in_specs=(
            P("y", nodes),
            P("y", None),
            P(nodes, None),
            P(nodes),
            P(nodes, None, None, None),
            P("y", nodes),
        ),
        out_specs=(P("y", nodes), P("y", None), P("y", nodes)),
        check_vma=False,
    )
```

```python
import jax
import jax.numpy as jnp
from jax import lax
from jax.experimental import pallas as pl
from jax.experimental.pallas import tpu as pltpu
from jax.sharding import Mesh, PartitionSpec as P

BF = jnp.bfloat16
F32 = jnp.float32
NZ, NW, NX, NC, NY = 8, 2, 4, 2, 4
NP = NW * NX
K, B, FL, HL = 16, 128, 32, 64
SMALL = HL + 16
RIDE = NC * FL + NC * HL + 2 * FL
D_AT, W_AT = NC * FL, NC * FL + NC * HL
C0, C1 = 0.7978845608, 0.044715
VM = pltpu.CompilerParams(vmem_limit_bytes=32 * 1024 * 1024)
VMEM = pl.BlockSpec(memory_space=pltpu.VMEM)
SMEM = pl.BlockSpec(memory_space=pltpu.SMEM)


def dot(a, b, ca, cb):
    return lax.dot_general(a, b, (((ca,), (cb,)), ((), ())), preferred_element_type=F32)


def call(kernel, outs, name, ins, scratch=()):
    specs, args = zip(*ins)
    one = not isinstance(outs, list)
    shapes = [jax.ShapeDtypeStruct(*o) for o in ((outs,) if one else outs)]
    return pl.pallas_call(
        kernel,
        out_shape=shapes[0] if one else tuple(shapes),
        in_specs=list(specs),
        out_specs=VMEM if one else tuple(VMEM for _ in shapes),
        scratch_shapes=list(scratch),
        compiler_params=VM,
        name=name,
    )(*args)


def small_kernel(cols, count, d_out, out):
    lane = lax.broadcasted_iota(jnp.int32, (16, B), 1)
    meta = jnp.where(lane == K, count[0], 0)
    for s in range(K):
        meta = jnp.where(lane == s, cols[0, s], meta)
    out[0:HL, :] = d_out[...]
    out[HL:, :] = meta.astype(F32).astype(BF)


def agg_kernel(small, other, mine, peer, xg, out, idx, ints, sem):
    core = lax.axis_index("c")
    for r, got in enumerate((small, other)):
        idx[r] = got[HL:, :].astype(F32)[0:8].astype(jnp.int32)
    copy = pltpu.make_async_copy(idx, ints, sem)
    copy.start()
    copy.wait()
    for r, blocks in enumerate((mine, peer)):
        acc = jnp.zeros((FL, B), F32)
        for s in range(K):
            owner = ints[r, 0, s]
            use = jnp.logical_and(owner % NC == core, s < ints[r, 0, K])
            got = xg[(owner // NC) % NP, owner // (NC * NP)]
            got = jnp.where(use, got, jnp.zeros_like(got))
            acc = acc + dot(got, blocks[s * B : (s + 1) * B, :], 1, 1)
        out[r] = acc


def ride_kernel(parts, small, other, weight, out):
    core = lax.axis_index("c")
    for y in range(NY):
        out[y, W_AT : W_AT + FL, :] = weight[:, :B]
        out[y, W_AT + FL :, :] = weight[:, B:]
    for c in range(NC):
        agg = (parts[c, 0] + parts[1 - c, 1]).astype(BF)
        cot = jnp.where(core == c, small[0:HL, :].astype(F32), other[0:HL, :].astype(F32))
        for y in range(NY):
            out[y, c * FL : (c + 1) * FL, :] = agg
            out[y, D_AT + c * HL : D_AT + (c + 1) * HL, :] = cot.astype(BF)


def back_kernel(idx, got, mine, peer, out_t, out, term, hidden):
    core, y_at = lax.axis_index("c"), lax.axis_index("y")
    term[...] = jnp.zeros_like(term)
    agg = jnp.concatenate(
        [
            jnp.concatenate([got[y, c * FL : (c + 1) * FL, :] for y in range(NY)], axis=0)
            for c in range(NC)
        ],
        axis=1,
    )
    own = jnp.concatenate([got[y_at, c * FL : (c + 1) * FL, :] for c in range(NC)], axis=1)
    back = jnp.zeros((FL, NC * B), F32)
    for h in range(2):
        rows = slice(W_AT + h * FL, W_AT + (h + 1) * FL)
        w = jnp.concatenate([got[y, rows, :] for y in range(NY)], axis=0)
        pre = dot(w, agg, 0, 0)
        t = jnp.tanh(C0 * (pre + C1 * (pre * pre * pre)))
        val = (0.5 * pre * (1.0 + t)).astype(BF)
        der = 0.5 * (1.0 + t) + 0.5 * pre * (1.0 - t * t) * (C0 * (1.0 + 3.0 * C1 * (pre * pre)))
        for c in range(NC):
            for q in range(2):

                @pl.when(jnp.logical_and(core == c, y_at == 2 * h + q))
                def _():
                    out_t[...] = val[q * HL : (q + 1) * HL, c * B : (c + 1) * B]

        cot = jnp.concatenate(
            [
                jnp.concatenate(
                    [got[2 * h + q, D_AT + c * HL : D_AT + (c + 1) * HL, :] for q in range(2)],
                    axis=0,
                )
                for c in range(NC)
            ],
            axis=1,
        )
        grad = (cot.astype(F32) * der).astype(BF)
        hidden[h] = grad
        back = back + dot(got[y_at, rows, :], grad, 1, 0)
    gw = dot(own, hidden[core], 1, 1).astype(BF)
    back = back.astype(BF)
    for r, blocks in enumerate((mine, peer)):
        mix = back[:, :B], back[:, B:]
        first = core == 0 if r == 0 else core == 1
        grad = jnp.where(first, mix[0], mix[1])
        for s in range(K):
            owner = idx[r, 0, s]
            use = jnp.logical_and(owner % NC == core, s < idx[r, 0, K])
            at = ((owner // NC) % NP) * NZ + owner // (NC * NP)
            at = jnp.where(use, at, NP * NZ)
            term[at] = term[at] + dot(grad, blocks[s * B : (s + 1) * B, :], 1, 0)
    for x in range(NP):
        for z in range(NZ):
            out[x, z * FL : (z + 1) * FL, :] = term[x * NZ + z].astype(BF)
        out[x, NZ * FL :, :] = gw


def sum_kernel(got, out):
    gw = sum(got[x, NZ * FL :, :].astype(F32) for x in range(NP)).astype(BF)
    for z in range(NZ):
        rows = slice(z * FL, (z + 1) * FL)
        out[z, 0:FL, :] = sum(got[x, rows, :].astype(F32) for x in range(NP)).astype(BF)
        out[z, FL:, :] = gw


def half_kernel(got, out):
    out[...] = sum(got[z, FL:, :].astype(F32) for z in range(NZ))


def last_kernel(got, halves, grad_w, grad_x):
    grad_w[:, :B] = halves[0]
    grad_w[:, B:] = halves[1]
    grad_x[...] = sum(got[z, 0:FL, :].astype(F32) for z in range(NZ))


def local(x_t, weight, block_cols, block_count, block_vals, d_out_t):
    mine = block_vals.reshape(K * B, B)
    with jax.named_scope("gather_x"):
        a = lax.all_to_all(jnp.broadcast_to(x_t, (NZ, FL, B)), "z", 0, 0, tiled=True)
    small = call(
        small_kernel,
        ((SMALL, B), BF),
        "small",
        [(SMEM, block_cols), (SMEM, block_count), (VMEM, d_out_t)],
    )
    with jax.named_scope("swap_core"):
        peer = lax.ppermute(mine, "c", [(0, 1), (1, 0)])
        other = lax.ppermute(small, "c", [(0, 1), (1, 0)])
    with jax.named_scope("gather_x"):
        a = lax.all_to_all(jnp.broadcast_to(a, (NP, NZ, FL, B)), ("w", "x"), 0, 0, tiled=True)
    parts, idx = call(
        agg_kernel,
        [((NC, FL, B), F32), ((NC, 8, B), jnp.int32)],
        "agg",
        [(VMEM, small), (VMEM, other), (VMEM, mine), (VMEM, peer), (VMEM, a)],
        [pltpu.SMEM((NC, 8, B), jnp.int32), pltpu.SemaphoreType.DMA],
    )
    with jax.named_scope("pair_agg"):
        parts = lax.all_gather(parts, "c", axis=0, tiled=False)
    ride = call(
        ride_kernel,
        ((NY, RIDE, B), BF),
        "ride",
        [(VMEM, parts), (VMEM, small), (VMEM, other), (VMEM, weight)],
    )
    with jax.named_scope("share_agg"):
        ride = lax.all_to_all(ride, "y", 0, 0, tiled=True)
    out_t, term = call(
        back_kernel,
        [((HL, B), BF), ((NP, NZ * FL + FL, B), BF)],
        "back",
        [(SMEM, idx), (VMEM, ride), (VMEM, mine), (VMEM, peer)],
        [pltpu.VMEM((NP * NZ + 1, FL, B), F32), pltpu.VMEM((2, B, NC * B), BF)],
    )
    with jax.named_scope("scatter_x"):
        term = lax.all_to_all(term, ("w", "x"), 0, 0, tiled=True)
    term = call(sum_kernel, ((NZ, 2 * FL, B), BF), "sum_x", [(VMEM, term)])
    with jax.named_scope("scatter_z"):
        term = lax.all_to_all(term, "z", 0, 0, tiled=True)
    half = call(half_kernel, ((FL, B), F32), "half", [(VMEM, term)])
    with jax.named_scope("join_w"):
        halves = lax.all_gather(half, "c", axis=0, tiled=False)
    grad_w, grad_x = call(
        last_kernel,
        [((FL, 2 * B), F32), ((FL, B), F32)],
        "last",
        [(VMEM, term), (VMEM, halves)],
    )
    return (out_t, grad_w, grad_x)


def solution(mesh):
    fine = Mesh(mesh.devices.reshape(NZ, NW, NX, NC, NY), ("z", "w", "x", "c", "y"))
    nodes = ("z", "w", "x", "c")
    return jax.shard_map(
        local,
        mesh=fine,
        in_specs=(
            P("y", nodes),
            P("y", None),
            P(nodes, None),
            P(nodes),
            P(nodes, None, None, None),
            P("y", nodes),
        ),
        out_specs=(P("y", nodes), P("y", None), P("y", nodes)),
        check_vma=False,
    )
```

```python
import jax
import jax.numpy as jnp
from jax import lax
from jax.experimental import pallas as pl
from jax.experimental.pallas import tpu as pltpu
from jax.sharding import Mesh, PartitionSpec as P

BF = jnp.bfloat16
F32 = jnp.float32
NZ, NW, NX, NC, NY = 8, 2, 4, 2, 4
NP = NW * NX
K, B, FL, HL = 16, 128, 32, 64
D_OUT, META, MINE = K * B, K * B + HL, K * B + HL + 16
RIDE = NC * FL + NC * HL + 2 * FL
C_AT, W_AT = NC * FL, NC * FL + NC * HL
C0, C1 = 0.7978845608, 0.044715
VM = pltpu.CompilerParams(vmem_limit_bytes=32 * 1024 * 1024)
VMEM = pl.BlockSpec(memory_space=pltpu.VMEM)
SMEM = pl.BlockSpec(memory_space=pltpu.SMEM)
HBM = pl.BlockSpec(memory_space=pl.ANY)


def dot(a, b, ca, cb):
    return lax.dot_general(a, b, (((ca,), (cb,)), ((), ())), preferred_element_type=F32)


def call(kernel, outs, name, ins, scratch=()):
    specs, args = zip(*ins)
    one = not isinstance(outs, list)
    shapes = [jax.ShapeDtypeStruct(*o) for o in ((outs,) if one else outs)]
    return pl.pallas_call(
        kernel,
        out_shape=shapes[0] if one else tuple(shapes),
        in_specs=list(specs),
        out_specs=VMEM if one else tuple(VMEM for _ in shapes),
        scratch_shapes=list(scratch),
        compiler_params=VM,
        name=name,
    )(*args)


def pack_kernel(meta, d_out, vals, mine, sems):
    parts = ((vals, mine.at[0:D_OUT]), (d_out, mine.at[D_OUT:META]))
    copies = [pltpu.make_async_copy(*part, sems.at[i]) for i, part in enumerate(parts)]
    for copy in copies:
        copy.start()
    mine[META:, :] = meta[...].astype(F32).astype(BF)
    for copy in copies:
        copy.wait()


def agg_kernel(mine, peer, xg, out, idx, ints, sem):
    core = lax.axis_index("c")
    for r, got in enumerate((mine, peer)):
        idx[r] = got[META:, :].astype(F32)[0:8].astype(jnp.int32)
    copy = pltpu.make_async_copy(idx, ints, sem)
    copy.start()
    copy.wait()
    for r, blocks in enumerate((mine, peer)):
        acc = jnp.zeros((FL, B), F32)
        for s in range(K):
            owner = ints[r, 0, s]
            use = jnp.logical_and(owner % NC == core, s < ints[r, 0, K])
            got = xg[(owner // NC) % NP, owner // (NC * NP)]
            got = jnp.where(use, got, jnp.zeros_like(got))
            acc = acc + dot(got, blocks[s * B : (s + 1) * B, :], 1, 1)
        out[r] = acc


def ride_kernel(parts, mine, peer, weight, out):
    core = lax.axis_index("c")
    for y in range(NY):
        out[y, W_AT : W_AT + FL, :] = weight[:, :B]
        out[y, W_AT + FL :, :] = weight[:, B:]
    for c in range(NC):
        agg = (parts[c, 0] + parts[1 - c, 1]).astype(BF)
        cot = [got[D_OUT:META, :].astype(F32) for got in (mine, peer)]
        cot = jnp.where(core == c, *cot)
        for y in range(NY):
            out[y, c * FL : (c + 1) * FL, :] = agg
            out[y, C_AT + c * HL : C_AT + (c + 1) * HL, :] = cot.astype(BF)


def back_kernel(idx, got, mine, peer, out_t, out, term, hidden):
    core, y_at = lax.axis_index("c"), lax.axis_index("y")
    term[...] = jnp.zeros_like(term)
    agg = jnp.concatenate(
        [
            jnp.concatenate([got[y, c * FL : (c + 1) * FL, :] for y in range(NY)], axis=0)
            for c in range(NC)
        ],
        axis=1,
    )
    own = jnp.concatenate([got[y_at, c * FL : (c + 1) * FL, :] for c in range(NC)], axis=1)
    back = jnp.zeros((FL, NC * B), F32)
    for h in range(2):
        rows = slice(W_AT + h * FL, W_AT + (h + 1) * FL)
        w = jnp.concatenate([got[y, rows, :] for y in range(NY)], axis=0)
        pre = dot(w, agg, 0, 0)
        t = jnp.tanh(C0 * (pre + C1 * (pre * pre * pre)))
        val = (0.5 * pre * (1.0 + t)).astype(BF)
        der = 0.5 * (1.0 + t) + 0.5 * pre * (1.0 - t * t) * (C0 * (1.0 + 3.0 * C1 * (pre * pre)))
        for c in range(NC):
            for q in range(2):

                @pl.when(jnp.logical_and(core == c, y_at == 2 * h + q))
                def _():
                    out_t[...] = val[q * HL : (q + 1) * HL, c * B : (c + 1) * B]

        cot = jnp.concatenate(
            [
                jnp.concatenate(
                    [got[2 * h + q, C_AT + c * HL : C_AT + (c + 1) * HL, :] for q in range(2)],
                    axis=0,
                )
                for c in range(NC)
            ],
            axis=1,
        )
        grad = (cot.astype(F32) * der).astype(BF)
        hidden[h] = grad
        back = back + dot(got[y_at, rows, :], grad, 1, 0)
    gw = dot(own, hidden[core], 1, 1).astype(BF)
    back = back.astype(BF)
    for r, blocks in enumerate((mine, peer)):
        mix = back[:, :B], back[:, B:]
        first = core == 0 if r == 0 else core == 1
        grad = jnp.where(first, mix[0], mix[1])
        for s in range(K):
            owner = idx[r, 0, s]
            use = jnp.logical_and(owner % NC == core, s < idx[r, 0, K])
            at = ((owner // NC) % NP) * NZ + owner // (NC * NP)
            at = jnp.where(use, at, NP * NZ)
            term[at] = term[at] + dot(grad, blocks[s * B : (s + 1) * B, :], 1, 0)
    for x in range(NP):
        for z in range(NZ):
            out[x, z * FL : (z + 1) * FL, :] = term[x * NZ + z].astype(BF)
        out[x, NZ * FL :, :] = gw


def sum_kernel(got, out):
    gw = sum(got[x, NZ * FL :, :].astype(F32) for x in range(NP)).astype(BF)
    for z in range(NZ):
        rows = slice(z * FL, (z + 1) * FL)
        out[z, 0:FL, :] = sum(got[x, rows, :].astype(F32) for x in range(NP)).astype(BF)
        out[z, FL:, :] = gw


def half_kernel(got, out):
    out[...] = sum(got[z, FL:, :].astype(F32) for z in range(NZ))


def last_kernel(got, halves, grad_w, grad_x):
    grad_w[:, :B] = halves[0]
    grad_w[:, B:] = halves[1]
    grad_x[...] = sum(got[z, 0:FL, :].astype(F32) for z in range(NZ))


def local(x_t, weight, block_cols, block_count, block_vals, d_out_t):
    with jax.named_scope("gather_x"):
        a = lax.all_to_all(jnp.broadcast_to(x_t, (NZ, FL, B)), "z", 0, 0, tiled=True)
    meta = jnp.concatenate([block_cols, block_count[:, None]], axis=1)
    mine = call(
        pack_kernel,
        ((MINE, B), BF),
        "pack",
        [
            (VMEM, jnp.pad(meta, ((0, 15), (0, B - K - 1)))),
            (HBM, d_out_t),
            (HBM, block_vals.reshape(K * B, B)),
        ],
        [pltpu.SemaphoreType.DMA((2,))],
    )
    with jax.named_scope("swap_core"):
        peer = lax.ppermute(mine, "c", [(0, 1), (1, 0)])
    with jax.named_scope("gather_x"):
        a = lax.all_to_all(jnp.broadcast_to(a, (NP, NZ, FL, B)), ("w", "x"), 0, 0, tiled=True)
    parts, idx = call(
        agg_kernel,
        [((NC, FL, B), F32), ((NC, 8, B), jnp.int32)],
        "agg",
        [(VMEM, mine), (VMEM, peer), (VMEM, a)],
        [pltpu.SMEM((NC, 8, B), jnp.int32), pltpu.SemaphoreType.DMA],
    )
    with jax.named_scope("pair_agg"):
        parts = lax.all_gather(parts, "c", axis=0, tiled=False)
    ride = call(
        ride_kernel,
        ((NY, RIDE, B), BF),
        "ride",
        [(VMEM, parts), (VMEM, mine), (VMEM, peer), (VMEM, weight)],
    )
    with jax.named_scope("share_agg"):
        ride = lax.all_to_all(ride, "y", 0, 0, tiled=True)
    out_t, term = call(
        back_kernel,
        [((HL, B), BF), ((NP, NZ * FL + FL, B), BF)],
        "back",
        [(SMEM, idx), (VMEM, ride), (VMEM, mine), (VMEM, peer)],
        [pltpu.VMEM((NP * NZ + 1, FL, B), F32), pltpu.VMEM((2, B, NC * B), BF)],
    )
    with jax.named_scope("scatter_x"):
        term = lax.all_to_all(term, ("w", "x"), 0, 0, tiled=True)
    term = call(sum_kernel, ((NZ, 2 * FL, B), BF), "sum_x", [(VMEM, term)])
    with jax.named_scope("scatter_z"):
        term = lax.all_to_all(term, "z", 0, 0, tiled=True)
    half = call(half_kernel, ((FL, B), F32), "half", [(VMEM, term)])
    with jax.named_scope("join_w"):
        halves = lax.all_gather(half, "c", axis=0, tiled=False)
    grad_w, grad_x = call(
        last_kernel,
        [((FL, 2 * B), F32), ((FL, B), F32)],
        "last",
        [(VMEM, term), (VMEM, halves)],
    )
    return (out_t, grad_w, grad_x)


def solution(mesh):
    fine = Mesh(mesh.devices.reshape(NZ, NW, NX, NC, NY), ("z", "w", "x", "c", "y"))
    nodes = ("z", "w", "x", "c")
    return jax.shard_map(
        local,
        mesh=fine,
        in_specs=(
            P("y", nodes),
            P("y", None),
            P(nodes, None),
            P(nodes),
            P(nodes, None, None, None),
            P("y", nodes),
        ),
        out_specs=(P("y", nodes), P("y", None), P("y", nodes)),
        check_vma=False,
    )
```

```python
import jax
import jax.numpy as jnp
from jax import lax
from jax.experimental import pallas as pl
from jax.experimental.pallas import tpu as pltpu
from jax.sharding import Mesh, PartitionSpec as P

BF = jnp.bfloat16
F32 = jnp.float32
NZ, NW, NX, NC, NY = 8, 2, 4, 2, 4
NP = NW * NX
K, B, FL, HL = 16, 128, 32, 64
D_OUT, META, MINE = K * B, K * B + HL, K * B + HL + 16
RIDE = NC * FL + NC * HL + 2 * FL
C_AT, W_AT = NC * FL, NC * FL + NC * HL
C0, C1 = 0.7978845608, 0.044715
VM = pltpu.CompilerParams(vmem_limit_bytes=32 * 1024 * 1024)
VMEM = pl.BlockSpec(memory_space=pltpu.VMEM)
SMEM = pl.BlockSpec(memory_space=pltpu.SMEM)
HBM = pl.BlockSpec(memory_space=pl.ANY)


def dot(a, b, ca, cb):
    return lax.dot_general(a, b, (((ca,), (cb,)), ((), ())), preferred_element_type=F32)


def call(kernel, outs, name, ins, scratch=()):
    specs, args = zip(*ins)
    one = not isinstance(outs, list)
    shapes = [jax.ShapeDtypeStruct(*o) for o in ((outs,) if one else outs)]
    return pl.pallas_call(
        kernel,
        out_shape=shapes[0] if one else tuple(shapes),
        in_specs=list(specs),
        out_specs=VMEM if one else tuple(VMEM for _ in shapes),
        scratch_shapes=list(scratch),
        compiler_params=VM,
        name=name,
    )(*args)


def pack_kernel(meta, d_out, vals, mine, sems):
    parts = ((vals, mine.at[0:D_OUT]), (d_out, mine.at[D_OUT:META]))
    copies = [pltpu.make_async_copy(*part, sems.at[i]) for i, part in enumerate(parts)]
    for copy in copies:
        copy.start()
    mine[META:, :] = meta[...].astype(F32).astype(BF)
    for copy in copies:
        copy.wait()


def agg_kernel(my_idx, peer_idx, mine, peer, xg, out):
    core = lax.axis_index("c")
    for r, (idx, blocks) in enumerate(((my_idx, mine), (peer_idx, peer))):
        acc = jnp.zeros((FL, B), F32)
        for s in range(K):
            owner = idx[s]
            use = jnp.logical_and(owner % NC == core, s < idx[K])
            got = xg[(owner // NC) % NP, owner // (NC * NP)]
            got = jnp.where(use, got, jnp.zeros_like(got))
            acc = acc + dot(got, blocks[s * B : (s + 1) * B, :], 1, 1)
        out[r] = acc


def ride_kernel(parts, mine, peer, weight, out):
    core = lax.axis_index("c")
    for y in range(NY):
        out[y, W_AT : W_AT + FL, :] = weight[:, :B]
        out[y, W_AT + FL :, :] = weight[:, B:]
    for c in range(NC):
        agg = (parts[c, 0] + parts[1 - c, 1]).astype(BF)
        cot = [got[D_OUT:META, :].astype(F32) for got in (mine, peer)]
        cot = jnp.where(core == c, *cot)
        for y in range(NY):
            out[y, c * FL : (c + 1) * FL, :] = agg
            out[y, C_AT + c * HL : C_AT + (c + 1) * HL, :] = cot.astype(BF)


def back_kernel(idx_a, idx_b, got, mine, peer, out_t, out, term, hidden, my_idx, peer_idx, sems):
    copies = [
        pltpu.make_async_copy(src, dst, sems.at[i])
        for i, (src, dst) in enumerate(((idx_a, my_idx), (idx_b, peer_idx)))
    ]
    for copy in copies:
        copy.start()
    core, y_at = lax.axis_index("c"), lax.axis_index("y")
    term[...] = jnp.zeros_like(term)
    agg = jnp.concatenate(
        [
            jnp.concatenate([got[y, c * FL : (c + 1) * FL, :] for y in range(NY)], axis=0)
            for c in range(NC)
        ],
        axis=1,
    )
    own = jnp.concatenate([got[y_at, c * FL : (c + 1) * FL, :] for c in range(NC)], axis=1)
    back = jnp.zeros((FL, NC * B), F32)
    for h in range(2):
        rows = slice(W_AT + h * FL, W_AT + (h + 1) * FL)
        w = jnp.concatenate([got[y, rows, :] for y in range(NY)], axis=0)
        pre = dot(w, agg, 0, 0)
        t = jnp.tanh(C0 * (pre + C1 * (pre * pre * pre)))
        val = (0.5 * pre * (1.0 + t)).astype(BF)
        der = 0.5 * (1.0 + t) + 0.5 * pre * (1.0 - t * t) * (C0 * (1.0 + 3.0 * C1 * (pre * pre)))
        for c in range(NC):
            for q in range(2):

                @pl.when(jnp.logical_and(core == c, y_at == 2 * h + q))
                def _():
                    out_t[...] = val[q * HL : (q + 1) * HL, c * B : (c + 1) * B]

        cot = jnp.concatenate(
            [
                jnp.concatenate(
                    [got[2 * h + q, C_AT + c * HL : C_AT + (c + 1) * HL, :] for q in range(2)],
                    axis=0,
                )
                for c in range(NC)
            ],
            axis=1,
        )
        grad = (cot.astype(F32) * der).astype(BF)
        hidden[h] = grad
        back = back + dot(got[y_at, rows, :], grad, 1, 0)
    gw = dot(own, hidden[core], 1, 1).astype(BF)
    back = back.astype(BF)
    for copy in copies:
        copy.wait()
    for r, (idx, blocks) in enumerate(((my_idx, mine), (peer_idx, peer))):
        mix = back[:, :B], back[:, B:]
        first = core == 0 if r == 0 else core == 1
        grad = jnp.where(first, mix[0], mix[1])
        for s in range(K):
            owner = idx[s]
            use = jnp.logical_and(owner % NC == core, s < idx[K])
            at = ((owner // NC) % NP) * NZ + owner // (NC * NP)
            at = jnp.where(use, at, NP * NZ)
            term[at] = term[at] + dot(grad, blocks[s * B : (s + 1) * B, :], 1, 0)
    for x in range(NP):
        for z in range(NZ):
            out[x, z * FL : (z + 1) * FL, :] = term[x * NZ + z].astype(BF)
        out[x, NZ * FL :, :] = gw


def sum_kernel(got, out):
    gw = sum(got[x, NZ * FL :, :].astype(F32) for x in range(NP)).astype(BF)
    for z in range(NZ):
        rows = slice(z * FL, (z + 1) * FL)
        out[z, 0:FL, :] = sum(got[x, rows, :].astype(F32) for x in range(NP)).astype(BF)
        out[z, FL:, :] = gw


def half_kernel(got, out):
    out[...] = sum(got[z, FL:, :].astype(F32) for z in range(NZ))


def last_kernel(got, halves, grad_w, grad_x):
    grad_w[:, :B] = halves[0]
    grad_w[:, B:] = halves[1]
    grad_x[...] = sum(got[z, 0:FL, :].astype(F32) for z in range(NZ))


def local(x_t, weight, block_cols, block_count, block_vals, d_out_t):
    with jax.named_scope("gather_x"):
        a = lax.all_to_all(jnp.broadcast_to(x_t, (NZ, FL, B)), "z", 0, 0, tiled=True)
    meta = jnp.concatenate([block_cols, block_count[:, None]], axis=1)
    mine = call(
        pack_kernel,
        ((MINE, B), BF),
        "pack",
        [
            (VMEM, jnp.pad(meta, ((0, 15), (0, B - K - 1)))),
            (HBM, d_out_t),
            (HBM, block_vals.reshape(K * B, B)),
        ],
        [pltpu.SemaphoreType.DMA((2,))],
    )
    with jax.named_scope("swap_core"):
        peer = lax.ppermute(mine, "c", [(0, 1), (1, 0)])
    with jax.named_scope("gather_x"):
        a = lax.all_to_all(jnp.broadcast_to(a, (NP, NZ, FL, B)), ("w", "x"), 0, 0, tiled=True)
    my_idx = meta[0]
    peer_idx = peer[META, : K + 1].astype(jnp.int32)
    parts = call(
        agg_kernel,
        ((NC, FL, B), F32),
        "agg",
        [(SMEM, my_idx), (SMEM, peer_idx), (VMEM, mine), (VMEM, peer), (VMEM, a)],
    )
    with jax.named_scope("pair_agg"):
        parts = lax.all_gather(parts, "c", axis=0, tiled=False)
    ride = call(
        ride_kernel,
        ((NY, RIDE, B), BF),
        "ride",
        [(VMEM, parts), (VMEM, mine), (VMEM, peer), (VMEM, weight)],
    )
    with jax.named_scope("share_agg"):
        ride = lax.all_to_all(ride, "y", 0, 0, tiled=True)
    out_t, term = call(
        back_kernel,
        [((HL, B), BF), ((NP, NZ * FL + FL, B), BF)],
        "back",
        [(HBM, my_idx), (HBM, peer_idx), (VMEM, ride), (VMEM, mine), (VMEM, peer)],
        [pltpu.VMEM((NP * NZ + 1, FL, B), F32), pltpu.VMEM((2, B, NC * B), BF)]
        + [pltpu.SMEM((K + 1,), jnp.int32)] * 2
        + [pltpu.SemaphoreType.DMA((2,))],
    )
    with jax.named_scope("scatter_x"):
        term = lax.all_to_all(term, ("w", "x"), 0, 0, tiled=True)
    term = call(sum_kernel, ((NZ, 2 * FL, B), BF), "sum_x", [(VMEM, term)])
    with jax.named_scope("scatter_z"):
        term = lax.all_to_all(term, "z", 0, 0, tiled=True)
    half = call(half_kernel, ((FL, B), F32), "half", [(VMEM, term)])
    with jax.named_scope("join_w"):
        halves = lax.all_gather(half, "c", axis=0, tiled=False)
    grad_w, grad_x = call(
        last_kernel,
        [((FL, 2 * B), F32), ((FL, B), F32)],
        "last",
        [(VMEM, term), (VMEM, halves)],
    )
    return (out_t, grad_w, grad_x)


def solution(mesh):
    fine = Mesh(mesh.devices.reshape(NZ, NW, NX, NC, NY), ("z", "w", "x", "c", "y"))
    nodes = ("z", "w", "x", "c")
    return jax.shard_map(
        local,
        mesh=fine,
        in_specs=(
            P("y", nodes),
            P("y", None),
            P(nodes, None),
            P(nodes),
            P(nodes, None, None, None),
            P("y", nodes),
        ),
        out_specs=(P("y", nodes), P("y", None), P("y", nodes)),
        check_vma=False,
    )
```

```python
import jax
import jax.numpy as jnp
from jax import lax
from jax.experimental import pallas as pl
from jax.experimental.pallas import tpu as pltpu
from jax.sharding import Mesh, PartitionSpec as P

BF = jnp.bfloat16
F32 = jnp.float32
NZ, NW, NX, NC, NY = 8, 2, 4, 2, 4
NP = NW * NX
K, B, FL, HL = 16, 128, 32, 64
D_OUT, META, MINE = K * B, K * B + HL, K * B + HL + 16
RIDE = NC * FL + NC * HL + 2 * FL
C_AT, W_AT = NC * FL, NC * FL + NC * HL
C0, C1 = 0.7978845608, 0.044715
VM = pltpu.CompilerParams(vmem_limit_bytes=32 * 1024 * 1024)
VMEM = pl.BlockSpec(memory_space=pltpu.VMEM)
SMEM = pl.BlockSpec(memory_space=pltpu.SMEM)
HBM = pl.BlockSpec(memory_space=pl.ANY)


def dot(a, b, ca, cb):
    return lax.dot_general(a, b, (((ca,), (cb,)), ((), ())), preferred_element_type=F32)


def call(kernel, outs, name, ins, scratch=(), spaces=None):
    specs, args = zip(*ins)
    one = not isinstance(outs, list)
    shapes = [jax.ShapeDtypeStruct(*o) for o in ((outs,) if one else outs)]
    return pl.pallas_call(
        kernel,
        out_shape=shapes[0] if one else tuple(shapes),
        in_specs=list(specs),
        out_specs=spaces or (VMEM if one else tuple(VMEM for _ in shapes)),
        scratch_shapes=list(scratch),
        compiler_params=VM,
        name=name,
    )(*args)


def pack_kernel(meta, d_out, vals, mine, sems):
    parts = ((vals, mine.at[0:D_OUT]), (d_out, mine.at[D_OUT:META]))
    copies = [pltpu.make_async_copy(*part, sems.at[i]) for i, part in enumerate(parts)]
    for copy in copies:
        copy.start()
    mine[META:, :] = meta[...].astype(F32).astype(BF)
    for copy in copies:
        copy.wait()


def agg_kernel(my_idx, peer_idx, mine, peer, xg, out):
    core = lax.axis_index("c")
    for r, (idx, blocks) in enumerate(((my_idx, mine), (peer_idx, peer))):
        acc = jnp.zeros((FL, B), F32)
        for s in range(0, K, 2):
            pair = []
            for q in range(s, s + 2):
                owner = idx[q]
                use = jnp.logical_and(owner % NC == core, q < idx[K])
                got = xg[(owner // NC) % NP, owner // (NC * NP)]
                pair.append(jnp.where(use, got, jnp.zeros_like(got)))
            vals = [blocks[q * B : (q + 1) * B, :] for q in range(s, s + 2)]
            acc = acc + dot(jnp.concatenate(pair, axis=1), jnp.concatenate(vals, axis=1), 1, 1)
        out[r] = acc


def ride_kernel(parts, mine, peer, weight, out):
    core = lax.axis_index("c")
    for y in range(NY):
        out[y, W_AT : W_AT + FL, :] = weight[:, :B]
        out[y, W_AT + FL :, :] = weight[:, B:]
    for c in range(NC):
        agg = (parts[c, 0] + parts[1 - c, 1]).astype(BF)
        cot = [got[D_OUT:META, :].astype(F32) for got in (mine, peer)]
        cot = jnp.where(core == c, *cot)
        for y in range(NY):
            out[y, c * FL : (c + 1) * FL, :] = agg
            out[y, C_AT + c * HL : C_AT + (c + 1) * HL, :] = cot.astype(BF)


def back_kernel(idx_a, idx_b, got, mine, peer, out_t, out, term, hidden, kept, my_idx, peer_idx, sems):
    copies = [
        pltpu.make_async_copy(src, dst, sems.at[i])
        for i, (src, dst) in enumerate(((idx_a, my_idx), (idx_b, peer_idx)))
    ]
    for copy in copies:
        copy.start()
    core, y_at = lax.axis_index("c"), lax.axis_index("y")
    term[...] = jnp.zeros_like(term)
    agg = jnp.concatenate(
        [
            jnp.concatenate([got[y, c * FL : (c + 1) * FL, :] for y in range(NY)], axis=0)
            for c in range(NC)
        ],
        axis=1,
    )
    own = jnp.concatenate([got[y_at, c * FL : (c + 1) * FL, :] for c in range(NC)], axis=1)
    back = jnp.zeros((FL, NC * B), F32)
    for h in range(2):
        rows = slice(W_AT + h * FL, W_AT + (h + 1) * FL)
        w = jnp.concatenate([got[y, rows, :] for y in range(NY)], axis=0)
        pre = dot(w, agg, 0, 0)
        t = jnp.tanh(C0 * (pre + C1 * (pre * pre * pre)))
        val = (0.5 * pre * (1.0 + t)).astype(BF)
        der = 0.5 * (1.0 + t) + 0.5 * pre * (1.0 - t * t) * (C0 * (1.0 + 3.0 * C1 * (pre * pre)))
        for c in range(NC):
            for q in range(2):

                @pl.when(jnp.logical_and(core == c, y_at == 2 * h + q))
                def _():
                    kept[...] = val[q * HL : (q + 1) * HL, c * B : (c + 1) * B]

        cot = jnp.concatenate(
            [
                jnp.concatenate(
                    [got[2 * h + q, C_AT + c * HL : C_AT + (c + 1) * HL, :] for q in range(2)],
                    axis=0,
                )
                for c in range(NC)
            ],
            axis=1,
        )
        grad = (cot.astype(F32) * der).astype(BF)
        hidden[h] = grad
        back = back + dot(got[y_at, rows, :], grad, 1, 0)
    leave = pltpu.make_async_copy(kept, out_t, sems.at[2])
    leave.start()
    gw = dot(own, hidden[core], 1, 1).astype(BF)
    back = back.astype(BF)
    for copy in copies:
        copy.wait()
    for r, (idx, blocks) in enumerate(((my_idx, mine), (peer_idx, peer))):
        mix = back[:, :B], back[:, B:]
        first = core == 0 if r == 0 else core == 1
        grad = jnp.where(first, mix[0], mix[1])
        for s in range(K):
            owner = idx[s]
            use = jnp.logical_and(owner % NC == core, s < idx[K])
            at = ((owner // NC) % NP) * NZ + owner // (NC * NP)
            at = jnp.where(use, at, NP * NZ)
            term[at] = term[at] + dot(grad, blocks[s * B : (s + 1) * B, :], 1, 0)
    for x in range(NP):
        for z in range(NZ):
            out[x, z * FL : (z + 1) * FL, :] = term[x * NZ + z].astype(BF)
        out[x, NZ * FL :, :] = gw
    leave.wait()


def sum_kernel(got, out):
    gw = sum(got[x, NZ * FL :, :].astype(F32) for x in range(NP)).astype(BF)
    for z in range(NZ):
        rows = slice(z * FL, (z + 1) * FL)
        out[z, 0:FL, :] = sum(got[x, rows, :].astype(F32) for x in range(NP)).astype(BF)
        out[z, FL:, :] = gw


def half_kernel(got, out):
    out[...] = sum(got[z, FL:, :].astype(F32) for z in range(NZ))


def last_kernel(got, halves, grad_w, grad_x):
    grad_w[:, :B] = halves[0]
    grad_w[:, B:] = halves[1]
    grad_x[...] = sum(got[z, 0:FL, :].astype(F32) for z in range(NZ))


def local(x_t, weight, block_cols, block_count, block_vals, d_out_t):
    with jax.named_scope("gather_x"):
        a = lax.all_to_all(jnp.broadcast_to(x_t, (NZ, FL, B)), "z", 0, 0, tiled=True)
    meta = jnp.concatenate([block_cols, block_count[:, None]], axis=1)
    mine = call(
        pack_kernel,
        ((MINE, B), BF),
        "pack",
        [
            (VMEM, jnp.pad(meta, ((0, 15), (0, B - K - 1)))),
            (HBM, d_out_t),
            (HBM, block_vals.reshape(K * B, B)),
        ],
        [pltpu.SemaphoreType.DMA((2,))],
    )
    with jax.named_scope("swap_core"):
        peer = lax.ppermute(mine, "c", [(0, 1), (1, 0)])
    with jax.named_scope("gather_x"):
        a = lax.all_to_all(jnp.broadcast_to(a, (NP, NZ, FL, B)), ("w", "x"), 0, 0, tiled=True)
    my_idx = meta[0]
    peer_idx = peer[META, : K + 1].astype(jnp.int32)
    parts = call(
        agg_kernel,
        ((NC, FL, B), F32),
        "agg",
        [(SMEM, my_idx), (SMEM, peer_idx), (VMEM, mine), (VMEM, peer), (VMEM, a)],
    )
    with jax.named_scope("pair_agg"):
        parts = lax.all_gather(parts, "c", axis=0, tiled=False)
    ride = call(
        ride_kernel,
        ((NY, RIDE, B), BF),
        "ride",
        [(VMEM, parts), (VMEM, mine), (VMEM, peer), (VMEM, weight)],
    )
    with jax.named_scope("share_agg"):
        ride = lax.all_to_all(ride, "y", 0, 0, tiled=True)
    out_t, term = call(
        back_kernel,
        [((HL, B), BF), ((NP, NZ * FL + FL, B), BF)],
        "back",
        [(HBM, my_idx), (HBM, peer_idx), (VMEM, ride), (VMEM, mine), (VMEM, peer)],
        [pltpu.VMEM((NP * NZ + 1, FL, B), F32), pltpu.VMEM((2, B, NC * B), BF)]
        + [pltpu.VMEM((HL, B), BF)]
        + [pltpu.SMEM((K + 1,), jnp.int32)] * 2
        + [pltpu.SemaphoreType.DMA((3,))],
        (HBM, VMEM),
    )
    with jax.named_scope("scatter_x"):
        term = lax.all_to_all(term, ("w", "x"), 0, 0, tiled=True)
    term = call(sum_kernel, ((NZ, 2 * FL, B), BF), "sum_x", [(VMEM, term)])
    with jax.named_scope("scatter_z"):
        term = lax.all_to_all(term, "z", 0, 0, tiled=True)
    half = call(half_kernel, ((FL, B), F32), "half", [(VMEM, term)])
    with jax.named_scope("join_w"):
        halves = lax.all_gather(half, "c", axis=0, tiled=False)
    grad_w, grad_x = call(
        last_kernel,
        [((FL, 2 * B), F32), ((FL, B), F32)],
        "last",
        [(VMEM, term), (VMEM, halves)],
    )
    return (out_t, grad_w, grad_x)


def solution(mesh):
    fine = Mesh(mesh.devices.reshape(NZ, NW, NX, NC, NY), ("z", "w", "x", "c", "y"))
    nodes = ("z", "w", "x", "c")
    return jax.shard_map(
        local,
        mesh=fine,
        in_specs=(
            P("y", nodes),
            P("y", None),
            P(nodes, None),
            P(nodes),
            P(nodes, None, None, None),
            P("y", nodes),
        ),
        out_specs=(P("y", nodes), P("y", None), P("y", nodes)),
        check_vma=False,
    )
```

```python
import jax
import jax.numpy as jnp
from jax import lax
from jax.experimental import pallas as pl
from jax.experimental.pallas import tpu as pltpu
from jax.sharding import Mesh, PartitionSpec as P

BF = jnp.bfloat16
F32 = jnp.float32
NZ, NW, NX, NC, NY = 8, 2, 4, 2, 4
NP = NW * NX
K, B, FL, HL = 16, 128, 32, 64
D_OUT, META, MINE = K * B, K * B + HL, K * B + HL + 16
RIDE = NC * FL + NC * HL + 2 * FL
C_AT, W_AT = NC * FL, NC * FL + NC * HL
C0, C1 = 0.7978845608, 0.044715
VM = pltpu.CompilerParams(vmem_limit_bytes=32 * 1024 * 1024)
VMEM = pl.BlockSpec(memory_space=pltpu.VMEM)
SMEM = pl.BlockSpec(memory_space=pltpu.SMEM)
HBM = pl.BlockSpec(memory_space=pl.ANY)


def dot(a, b, ca, cb):
    return lax.dot_general(a, b, (((ca,), (cb,)), ((), ())), preferred_element_type=F32)


def call(kernel, outs, name, ins, scratch=(), spaces=None):
    specs, args = zip(*ins)
    one = not isinstance(outs, list)
    shapes = [jax.ShapeDtypeStruct(*o) for o in ((outs,) if one else outs)]
    return pl.pallas_call(
        kernel,
        out_shape=shapes[0] if one else tuple(shapes),
        in_specs=list(specs),
        out_specs=spaces or (VMEM if one else tuple(VMEM for _ in shapes)),
        scratch_shapes=list(scratch),
        compiler_params=VM,
        name=name,
    )(*args)


def pack_kernel(meta, d_out, vals, mine, sems):
    parts = ((vals, mine.at[0:D_OUT]), (d_out, mine.at[D_OUT:META]))
    copies = [pltpu.make_async_copy(*part, sems.at[i]) for i, part in enumerate(parts)]
    for copy in copies:
        copy.start()
    mine[META:, :] = meta[...].astype(F32).astype(BF)
    for copy in copies:
        copy.wait()


def agg_kernel(my_idx, peer_idx, mine, peer, xg, out):
    core = lax.axis_index("c")
    for r, (idx, blocks) in enumerate(((my_idx, mine), (peer_idx, peer))):
        acc = jnp.zeros((FL, B), F32)
        for s in range(0, K, 2):
            pair = []
            for q in range(s, s + 2):
                owner = idx[q]
                use = jnp.logical_and(owner % NC == core, q < idx[K])
                got = xg[(owner // NC) % NP, owner // (NC * NP)]
                pair.append(jnp.where(use, got, jnp.zeros_like(got)))
            vals = [blocks[q * B : (q + 1) * B, :] for q in range(s, s + 2)]
            acc = acc + dot(jnp.concatenate(pair, axis=1), jnp.concatenate(vals, axis=1), 1, 1)
        out[r] = acc


def ride_kernel(parts, mine, peer, weight, out):
    core = lax.axis_index("c")
    for y in range(NY):
        out[y, W_AT : W_AT + FL, :] = weight[:, :B]
        out[y, W_AT + FL :, :] = weight[:, B:]
    for c in range(NC):
        agg = (parts[c, 0] + parts[1 - c, 1]).astype(BF)
        cot = [got[D_OUT:META, :].astype(F32) for got in (mine, peer)]
        cot = jnp.where(core == c, *cot)
        for y in range(NY):
            out[y, c * FL : (c + 1) * FL, :] = agg
            out[y, C_AT + c * HL : C_AT + (c + 1) * HL, :] = cot.astype(BF)


def back_kernel(idx_a, idx_b, got, mine, peer, out_t, out, term, hidden, kept, my_idx, peer_idx, sems):
    copies = [
        pltpu.make_async_copy(src, dst, sems.at[i])
        for i, (src, dst) in enumerate(((idx_a, my_idx), (idx_b, peer_idx)))
    ]
    for copy in copies:
        copy.start()
    core, y_at = lax.axis_index("c"), lax.axis_index("y")
    term[...] = jnp.zeros_like(term)
    agg = jnp.concatenate(
        [
            jnp.concatenate([got[y, c * FL : (c + 1) * FL, :] for y in range(NY)], axis=0)
            for c in range(NC)
        ],
        axis=1,
    )
    own = jnp.concatenate([got[y_at, c * FL : (c + 1) * FL, :] for c in range(NC)], axis=1)
    back = jnp.zeros((FL, NC * B), F32)
    for h in range(2):
        rows = slice(W_AT + h * FL, W_AT + (h + 1) * FL)
        w = jnp.concatenate([got[y, rows, :] for y in range(NY)], axis=0)
        pre = dot(w, agg, 0, 0)
        sq = pre * pre
        u = 0.5 + 0.5 * jnp.tanh(pre * (C0 + (C0 * C1) * sq))
        val = (pre * u).astype(BF)
        der = u + (pre * (u - u * u)) * (2.0 * C0 + (6.0 * C0 * C1) * sq)
        for c in range(NC):
            for q in range(2):

                @pl.when(jnp.logical_and(core == c, y_at == 2 * h + q))
                def _():
                    kept[...] = val[q * HL : (q + 1) * HL, c * B : (c + 1) * B]

        cot = jnp.concatenate(
            [
                jnp.concatenate(
                    [got[2 * h + q, C_AT + c * HL : C_AT + (c + 1) * HL, :] for q in range(2)],
                    axis=0,
                )
                for c in range(NC)
            ],
            axis=1,
        )
        grad = (cot.astype(F32) * der).astype(BF)
        hidden[h] = grad
        back = back + dot(got[y_at, rows, :], grad, 1, 0)
    leave = pltpu.make_async_copy(kept, out_t, sems.at[2])
    leave.start()
    gw = dot(own, hidden[core], 1, 1).astype(BF)
    back = back.astype(BF)
    for copy in copies:
        copy.wait()
    for r, (idx, blocks) in enumerate(((my_idx, mine), (peer_idx, peer))):
        mix = back[:, :B], back[:, B:]
        first = core == 0 if r == 0 else core == 1
        grad = jnp.where(first, mix[0], mix[1])
        for s in range(K):
            owner = idx[s]
            use = jnp.logical_and(owner % NC == core, s < idx[K])
            at = ((owner // NC) % NP) * NZ + owner // (NC * NP)
            at = jnp.where(use, at, NP * NZ)
            term[at] = term[at] + dot(grad, blocks[s * B : (s + 1) * B, :], 1, 0)
    for x in range(NP):
        for z in range(NZ):
            out[x, z * FL : (z + 1) * FL, :] = term[x * NZ + z].astype(BF)
        out[x, NZ * FL :, :] = gw
    leave.wait()


def sum_kernel(got, out):
    gw = sum(got[x, NZ * FL :, :].astype(F32) for x in range(NP)).astype(BF)
    for z in range(NZ):
        rows = slice(z * FL, (z + 1) * FL)
        out[z, 0:FL, :] = sum(got[x, rows, :].astype(F32) for x in range(NP)).astype(BF)
        out[z, FL:, :] = gw


def half_kernel(got, out):
    out[...] = sum(got[z, FL:, :].astype(F32) for z in range(NZ))


def last_kernel(got, halves, grad_w, grad_x):
    grad_w[:, :B] = halves[0]
    grad_w[:, B:] = halves[1]
    grad_x[...] = sum(got[z, 0:FL, :].astype(F32) for z in range(NZ))


def local(x_t, weight, block_cols, block_count, block_vals, d_out_t):
    with jax.named_scope("gather_x"):
        a = lax.all_to_all(jnp.broadcast_to(x_t, (NZ, FL, B)), "z", 0, 0, tiled=True)
    meta = jnp.concatenate([block_cols, block_count[:, None]], axis=1)
    mine = call(
        pack_kernel,
        ((MINE, B), BF),
        "pack",
        [
            (VMEM, jnp.pad(meta, ((0, 15), (0, B - K - 1)))),
            (HBM, d_out_t),
            (HBM, block_vals.reshape(K * B, B)),
        ],
        [pltpu.SemaphoreType.DMA((2,))],
    )
    with jax.named_scope("swap_core"):
        peer = lax.ppermute(mine, "c", [(0, 1), (1, 0)])
    with jax.named_scope("gather_x"):
        a = lax.all_to_all(jnp.broadcast_to(a, (NP, NZ, FL, B)), ("w", "x"), 0, 0, tiled=True)
    my_idx = meta[0]
    peer_idx = peer[META, : K + 1].astype(jnp.int32)
    parts = call(
        agg_kernel,
        ((NC, FL, B), F32),
        "agg",
        [(SMEM, my_idx), (SMEM, peer_idx), (VMEM, mine), (VMEM, peer), (VMEM, a)],
    )
    with jax.named_scope("pair_agg"):
        parts = lax.all_gather(parts, "c", axis=0, tiled=False)
    ride = call(
        ride_kernel,
        ((NY, RIDE, B), BF),
        "ride",
        [(VMEM, parts), (VMEM, mine), (VMEM, peer), (VMEM, weight)],
    )
    with jax.named_scope("share_agg"):
        ride = lax.all_to_all(ride, "y", 0, 0, tiled=True)
    out_t, term = call(
        back_kernel,
        [((HL, B), BF), ((NP, NZ * FL + FL, B), BF)],
        "back",
        [(HBM, my_idx), (HBM, peer_idx), (VMEM, ride), (VMEM, mine), (VMEM, peer)],
        [pltpu.VMEM((NP * NZ + 1, FL, B), F32), pltpu.VMEM((2, B, NC * B), BF)]
        + [pltpu.VMEM((HL, B), BF)]
        + [pltpu.SMEM((K + 1,), jnp.int32)] * 2
        + [pltpu.SemaphoreType.DMA((3,))],
        (HBM, VMEM),
    )
    with jax.named_scope("scatter_x"):
        term = lax.all_to_all(term, ("w", "x"), 0, 0, tiled=True)
    term = call(sum_kernel, ((NZ, 2 * FL, B), BF), "sum_x", [(VMEM, term)])
    with jax.named_scope("scatter_z"):
        term = lax.all_to_all(term, "z", 0, 0, tiled=True)
    half = call(half_kernel, ((FL, B), F32), "half", [(VMEM, term)])
    with jax.named_scope("join_w"):
        halves = lax.all_gather(half, "c", axis=0, tiled=False)
    grad_w, grad_x = call(
        last_kernel,
        [((FL, 2 * B), F32), ((FL, B), F32)],
        "last",
        [(VMEM, term), (VMEM, halves)],
    )
    return (out_t, grad_w, grad_x)


def solution(mesh):
    fine = Mesh(mesh.devices.reshape(NZ, NW, NX, NC, NY), ("z", "w", "x", "c", "y"))
    nodes = ("z", "w", "x", "c")
    return jax.shard_map(
        local,
        mesh=fine,
        in_specs=(
            P("y", nodes),
            P("y", None),
            P(nodes, None),
            P(nodes),
            P(nodes, None, None, None),
            P("y", nodes),
        ),
        out_specs=(P("y", nodes), P("y", None), P("y", nodes)),
        check_vma=False,
    )
```

```python
import jax
import jax.numpy as jnp
from jax import lax
from jax.experimental import pallas as pl
from jax.experimental.pallas import tpu as pltpu
from jax.sharding import Mesh, PartitionSpec as P

BF = jnp.bfloat16
F32 = jnp.float32
NZ, NW, NX, NC, NY = 8, 2, 4, 2, 4
NP = NW * NX
K, B, FL, HL = 16, 128, 32, 64
D_OUT, META, MINE = K * B, K * B + HL, K * B + HL + 16
RIDE = NC * FL + NC * HL + 2 * FL
C_AT, W_AT = NC * FL, NC * FL + NC * HL
C0, C1 = 0.7978845608, 0.044715
VM = pltpu.CompilerParams(vmem_limit_bytes=32 * 1024 * 1024)
VMEM = pl.BlockSpec(memory_space=pltpu.VMEM)
SMEM = pl.BlockSpec(memory_space=pltpu.SMEM)
HBM = pl.BlockSpec(memory_space=pl.ANY)


def dot(a, b, ca, cb):
    return lax.dot_general(a, b, (((ca,), (cb,)), ((), ())), preferred_element_type=F32)


def call(kernel, outs, name, ins, scratch=(), spaces=None):
    specs, args = zip(*ins)
    one = not isinstance(outs, list)
    shapes = [jax.ShapeDtypeStruct(*o) for o in ((outs,) if one else outs)]
    return pl.pallas_call(
        kernel,
        out_shape=shapes[0] if one else tuple(shapes),
        in_specs=list(specs),
        out_specs=spaces or (VMEM if one else tuple(VMEM for _ in shapes)),
        scratch_shapes=list(scratch),
        compiler_params=VM,
        name=name,
    )(*args)


def pack_kernel(meta, d_out, vals, mine, sems):
    parts = ((vals, mine.at[0:D_OUT]), (d_out, mine.at[D_OUT:META]))
    copies = [pltpu.make_async_copy(*part, sems.at[i]) for i, part in enumerate(parts)]
    for copy in copies:
        copy.start()
    mine[META:, :] = meta[...].astype(F32).astype(BF)
    for copy in copies:
        copy.wait()


def agg_kernel(my_idx, peer_idx, mine, peer, xg, out):
    core = lax.axis_index("c")
    for r, (idx, blocks) in enumerate(((my_idx, mine), (peer_idx, peer))):
        acc = jnp.zeros((FL, B), F32)
        for s in range(0, K, 2):
            pair = []
            for q in range(s, s + 2):
                owner = idx[q]
                use = jnp.logical_and(owner % NC == core, q < idx[K])
                got = xg[(owner // NC) % NP, owner // (NC * NP)]
                pair.append(jnp.where(use, got, jnp.zeros_like(got)))
            vals = [blocks[q * B : (q + 1) * B, :] for q in range(s, s + 2)]
            acc = acc + dot(jnp.concatenate(pair, axis=1), jnp.concatenate(vals, axis=1), 1, 1)
        out[r] = acc


def ride_kernel(parts, mine, peer, weight, out):
    core = lax.axis_index("c")
    for y in range(NY):
        out[y, W_AT : W_AT + FL, :] = weight[:, :B]
        out[y, W_AT + FL :, :] = weight[:, B:]
    for c in range(NC):
        agg = (parts[c, 0] + parts[1 - c, 1]).astype(BF)
        cot = [got[D_OUT:META, :].astype(F32) for got in (mine, peer)]
        cot = jnp.where(core == c, *cot)
        for y in range(NY):
            out[y, c * FL : (c + 1) * FL, :] = agg
            out[y, C_AT + c * HL : C_AT + (c + 1) * HL, :] = cot.astype(BF)


def back_kernel(idx_a, idx_b, got, mine, peer, out_t, out, term, hidden, kept, my_idx, peer_idx, sems):
    copies = [
        pltpu.make_async_copy(src, dst, sems.at[i])
        for i, (src, dst) in enumerate(((idx_a, my_idx), (idx_b, peer_idx)))
    ]
    for copy in copies:
        copy.start()
    core, y_at = lax.axis_index("c"), lax.axis_index("y")
    term[...] = jnp.zeros_like(term)
    agg = jnp.concatenate(
        [
            jnp.concatenate([got[y, c * FL : (c + 1) * FL, :] for y in range(NY)], axis=0)
            for c in range(NC)
        ],
        axis=1,
    )
    own = jnp.concatenate([got[y_at, c * FL : (c + 1) * FL, :] for c in range(NC)], axis=1)
    back = jnp.zeros((FL, NC * B), F32)
    for h in range(2):
        rows = slice(W_AT + h * FL, W_AT + (h + 1) * FL)
        w = jnp.concatenate([got[y, rows, :] for y in range(NY)], axis=0)
        pre = dot(w, agg, 0, 0)
        sq = pre * pre
        u = 0.5 + 0.5 * jnp.tanh(pre * (C0 + (C0 * C1) * sq))
        val = (pre * u).astype(BF)
        der = u + (pre * (u - u * u)) * (2.0 * C0 + (6.0 * C0 * C1) * sq)
        kept[h * B : (h + 1) * B, :] = val
        cot = jnp.concatenate(
            [
                jnp.concatenate(
                    [got[2 * h + q, C_AT + c * HL : C_AT + (c + 1) * HL, :] for q in range(2)],
                    axis=0,
                )
                for c in range(NC)
            ],
            axis=1,
        )
        grad = (cot.astype(F32) * der).astype(BF)
        hidden[h] = grad
        back = back + dot(got[y_at, rows, :], grad, 1, 0)
    rows = pl.ds(pl.multiple_of(y_at * HL, HL), HL)
    lanes = pl.ds(pl.multiple_of(core * B, B), B)
    leave = pltpu.make_async_copy(kept.at[rows, lanes], out_t, sems.at[2])
    leave.start()
    gw = dot(own, hidden[core], 1, 1).astype(BF)
    back = back.astype(BF)
    for copy in copies:
        copy.wait()
    for r, (idx, blocks) in enumerate(((my_idx, mine), (peer_idx, peer))):
        mix = back[:, :B], back[:, B:]
        first = core == 0 if r == 0 else core == 1
        grad = jnp.where(first, mix[0], mix[1])
        for s in range(K):
            owner = idx[s]
            use = jnp.logical_and(owner % NC == core, s < idx[K])
            at = ((owner // NC) % NP) * NZ + owner // (NC * NP)
            at = jnp.where(use, at, NP * NZ)
            term[at] = term[at] + dot(grad, blocks[s * B : (s + 1) * B, :], 1, 0)
    for x in range(NP):
        for z in range(NZ):
            out[x, z * FL : (z + 1) * FL, :] = term[x * NZ + z].astype(BF)
        out[x, NZ * FL :, :] = gw
    leave.wait()


def sum_kernel(got, out):
    gw = sum(got[x, NZ * FL :, :].astype(F32) for x in range(NP)).astype(BF)
    for z in range(NZ):
        rows = slice(z * FL, (z + 1) * FL)
        out[z, 0:FL, :] = sum(got[x, rows, :].astype(F32) for x in range(NP)).astype(BF)
        out[z, FL:, :] = gw


def half_kernel(got, out):
    out[...] = sum(got[z, FL:, :].astype(F32) for z in range(NZ))


def last_kernel(got, halves, grad_w, grad_x):
    grad_w[:, :B] = halves[0]
    grad_w[:, B:] = halves[1]
    grad_x[...] = sum(got[z, 0:FL, :].astype(F32) for z in range(NZ))


def local(x_t, weight, block_cols, block_count, block_vals, d_out_t):
    with jax.named_scope("gather_x"):
        a = lax.all_to_all(jnp.broadcast_to(x_t, (NZ, FL, B)), "z", 0, 0, tiled=True)
    meta = jnp.concatenate([block_cols, block_count[:, None]], axis=1)
    mine = call(
        pack_kernel,
        ((MINE, B), BF),
        "pack",
        [
            (VMEM, jnp.pad(meta, ((0, 15), (0, B - K - 1)))),
            (HBM, d_out_t),
            (HBM, block_vals.reshape(K * B, B)),
        ],
        [pltpu.SemaphoreType.DMA((2,))],
    )
    with jax.named_scope("swap_core"):
        peer = lax.ppermute(mine, "c", [(0, 1), (1, 0)])
    with jax.named_scope("gather_x"):
        a = lax.all_to_all(jnp.broadcast_to(a, (NP, NZ, FL, B)), ("w", "x"), 0, 0, tiled=True)
    my_idx = meta[0]
    peer_idx = peer[META, : K + 1].astype(jnp.int32)
    parts = call(
        agg_kernel,
        ((NC, FL, B), F32),
        "agg",
        [(SMEM, my_idx), (SMEM, peer_idx), (VMEM, mine), (VMEM, peer), (VMEM, a)],
    )
    with jax.named_scope("pair_agg"):
        parts = lax.all_gather(parts, "c", axis=0, tiled=False)
    ride = call(
        ride_kernel,
        ((NY, RIDE, B), BF),
        "ride",
        [(VMEM, parts), (VMEM, mine), (VMEM, peer), (VMEM, weight)],
    )
    with jax.named_scope("share_agg"):
        ride = lax.all_to_all(ride, "y", 0, 0, tiled=True)
    out_t, term = call(
        back_kernel,
        [((HL, B), BF), ((NP, NZ * FL + FL, B), BF)],
        "back",
        [(HBM, my_idx), (HBM, peer_idx), (VMEM, ride), (VMEM, mine), (VMEM, peer)],
        [pltpu.VMEM((NP * NZ + 1, FL, B), F32), pltpu.VMEM((2, B, NC * B), BF)]
        + [pltpu.VMEM((2 * B, NC * B), BF)]
        + [pltpu.SMEM((K + 1,), jnp.int32)] * 2
        + [pltpu.SemaphoreType.DMA((3,))],
        (HBM, VMEM),
    )
    with jax.named_scope("scatter_x"):
        term = lax.all_to_all(term, ("w", "x"), 0, 0, tiled=True)
    term = call(sum_kernel, ((NZ, 2 * FL, B), BF), "sum_x", [(VMEM, term)])
    with jax.named_scope("scatter_z"):
        term = lax.all_to_all(term, "z", 0, 0, tiled=True)
    half = call(half_kernel, ((FL, B), F32), "half", [(VMEM, term)])
    with jax.named_scope("join_w"):
        halves = lax.all_gather(half, "c", axis=0, tiled=False)
    grad_w, grad_x = call(
        last_kernel,
        [((FL, 2 * B), F32), ((FL, B), F32)],
        "last",
        [(VMEM, term), (VMEM, halves)],
    )
    return (out_t, grad_w, grad_x)


def solution(mesh):
    fine = Mesh(mesh.devices.reshape(NZ, NW, NX, NC, NY), ("z", "w", "x", "c", "y"))
    nodes = ("z", "w", "x", "c")
    return jax.shard_map(
        local,
        mesh=fine,
        in_specs=(
            P("y", nodes),
            P("y", None),
            P(nodes, None),
            P(nodes),
            P(nodes, None, None, None),
            P("y", nodes),
        ),
        out_specs=(P("y", nodes), P("y", None), P("y", nodes)),
        check_vma=False,
    )
```

```python
import jax
import jax.numpy as jnp
from jax import lax
from jax.experimental import pallas as pl
from jax.experimental.pallas import tpu as pltpu
from jax.sharding import Mesh, PartitionSpec as P

BF = jnp.bfloat16
F32 = jnp.float32
NZ, NW, NX, NC, NY = 8, 2, 4, 2, 4
NP = NW * NX
K, B, FL, HL = 16, 128, 32, 64
D_OUT, META, MINE = K * B, K * B + HL, K * B + HL + 16
RIDE = NC * FL + NC * HL + 2 * FL
C_AT, W_AT = NC * FL, NC * FL + NC * HL
C0, C1 = 0.7978845608, 0.044715
VM = pltpu.CompilerParams(vmem_limit_bytes=32 * 1024 * 1024)
VMEM = pl.BlockSpec(memory_space=pltpu.VMEM)
SMEM = pl.BlockSpec(memory_space=pltpu.SMEM)
HBM = pl.BlockSpec(memory_space=pl.ANY)


def dot(a, b, ca, cb):
    return lax.dot_general(a, b, (((ca,), (cb,)), ((), ())), preferred_element_type=F32)


def call(kernel, outs, name, ins, scratch=(), spaces=None):
    specs, args = zip(*ins)
    one = not isinstance(outs, list)
    shapes = [jax.ShapeDtypeStruct(*o) for o in ((outs,) if one else outs)]
    return pl.pallas_call(
        kernel,
        out_shape=shapes[0] if one else tuple(shapes),
        in_specs=list(specs),
        out_specs=spaces or (VMEM if one else tuple(VMEM for _ in shapes)),
        scratch_shapes=list(scratch),
        compiler_params=VM,
        name=name,
    )(*args)


def pack_kernel(meta, d_out, vals, mine, sems):
    parts = ((vals, mine.at[0:D_OUT]), (d_out, mine.at[D_OUT:META]))
    copies = [pltpu.make_async_copy(*part, sems.at[i]) for i, part in enumerate(parts)]
    for copy in copies:
        copy.start()
    mine[META:, :] = meta[...].astype(F32).astype(BF)
    for copy in copies:
        copy.wait()


def agg_kernel(my_idx, peer_idx, mine, peer, xg, out):
    core = lax.axis_index("c")
    for r, (idx, blocks) in enumerate(((my_idx, mine), (peer_idx, peer))):
        acc = jnp.zeros((FL, B), F32)
        for s in range(0, K, 2):
            pair = []
            for q in range(s, s + 2):
                owner = idx[q]
                use = jnp.logical_and(owner % NC == core, q < idx[K])
                got = xg[(owner // NC) % NP, owner // (NC * NP)]
                pair.append(jnp.where(use, got, jnp.zeros_like(got)))
            vals = [blocks[q * B : (q + 1) * B, :] for q in range(s, s + 2)]
            acc = acc + dot(jnp.concatenate(pair, axis=1), jnp.concatenate(vals, axis=1), 1, 1)
        out[r] = acc


def ride_kernel(parts, mine, peer, weight, out):
    core = lax.axis_index("c")
    for y in range(NY):
        out[y, W_AT : W_AT + FL, :] = weight[:, :B]
        out[y, W_AT + FL :, :] = weight[:, B:]
    for c in range(NC):
        agg = (parts[c, 0] + parts[1 - c, 1]).astype(BF)
        cot = [got[D_OUT:META, :].astype(F32) for got in (mine, peer)]
        cot = jnp.where(core == c, *cot)
        for y in range(NY):
            out[y, c * FL : (c + 1) * FL, :] = agg
            out[y, C_AT + c * HL : C_AT + (c + 1) * HL, :] = cot.astype(BF)


def back_kernel(idx_a, idx_b, got, mine, peer, out_t, out, term, hidden, kept, my_idx, peer_idx, sems):
    copies = [
        pltpu.make_async_copy(src, dst, sems.at[i])
        for i, (src, dst) in enumerate(((idx_a, my_idx), (idx_b, peer_idx)))
    ]
    for copy in copies:
        copy.start()
    core, y_at = lax.axis_index("c"), lax.axis_index("y")
    term[...] = jnp.zeros_like(term)
    agg = jnp.concatenate(
        [
            jnp.concatenate([got[y, c * FL : (c + 1) * FL, :] for y in range(NY)], axis=0)
            for c in range(NC)
        ],
        axis=1,
    )
    own = jnp.concatenate([got[y_at, c * FL : (c + 1) * FL, :] for c in range(NC)], axis=1)
    back = jnp.zeros((FL, NC * B), F32)
    for h in range(2):
        rows = slice(W_AT + h * FL, W_AT + (h + 1) * FL)
        w = jnp.concatenate([got[y, rows, :] for y in range(NY)], axis=0)
        pre = dot(w, agg, 0, 0)
        sq = pre * pre
        u = 0.5 + 0.5 * jnp.tanh(pre * (C0 + (C0 * C1) * sq))
        val = (pre * u).astype(BF)
        der = u + (pre * (u - u * u)) * (2.0 * C0 + (6.0 * C0 * C1) * sq)
        kept[h * B : (h + 1) * B, :] = val
        cot = jnp.concatenate(
            [
                jnp.concatenate(
                    [got[2 * h + q, C_AT + c * HL : C_AT + (c + 1) * HL, :] for q in range(2)],
                    axis=0,
                )
                for c in range(NC)
            ],
            axis=1,
        )
        grad = (cot.astype(F32) * der).astype(BF)
        hidden[h] = grad
        back = back + dot(got[y_at, rows, :], grad, 1, 0)
    rows = pl.ds(pl.multiple_of(y_at * HL, HL), HL)
    lanes = pl.ds(pl.multiple_of(core * B, B), B)
    leave = pltpu.make_async_copy(kept.at[rows, lanes], out_t, sems.at[2])
    leave.start()
    gw = dot(own, hidden[core], 1, 1).astype(BF)
    back = back.astype(BF)
    for copy in copies:
        copy.wait()
    for r, (idx, blocks) in enumerate(((my_idx, mine), (peer_idx, peer))):
        mix = back[:, :B], back[:, B:]
        first = core == 0 if r == 0 else core == 1
        grad = jnp.where(first, mix[0], mix[1])
        for s in range(K):
            owner = idx[s]
            use = jnp.logical_and(owner % NC == core, s < idx[K])
            at = ((owner // NC) % NP) * NZ + owner // (NC * NP)
            at = jnp.where(use, at, NP * NZ)
            new = dot(grad, blocks[s * B : (s + 1) * B, :], 1, 0)
            term[at] = new if r == 0 else term[at] + new
    for x in range(NP):
        for z in range(NZ):
            out[x, z * FL : (z + 1) * FL, :] = term[x * NZ + z].astype(BF)
        out[x, NZ * FL :, :] = gw
    leave.wait()


def sum_kernel(got, out):
    gw = sum(got[x, NZ * FL :, :].astype(F32) for x in range(NP)).astype(BF)
    for z in range(NZ):
        rows = slice(z * FL, (z + 1) * FL)
        out[z, 0:FL, :] = sum(got[x, rows, :].astype(F32) for x in range(NP)).astype(BF)
        out[z, FL:, :] = gw


def half_kernel(got, out):
    out[...] = sum(got[z, FL:, :].astype(F32) for z in range(NZ))


def last_kernel(got, halves, grad_w, grad_x):
    grad_w[:, :B] = halves[0]
    grad_w[:, B:] = halves[1]
    grad_x[...] = sum(got[z, 0:FL, :].astype(F32) for z in range(NZ))


def local(x_t, weight, block_cols, block_count, block_vals, d_out_t):
    with jax.named_scope("gather_x"):
        a = lax.all_to_all(jnp.broadcast_to(x_t, (NZ, FL, B)), "z", 0, 0, tiled=True)
    meta = jnp.concatenate([block_cols, block_count[:, None]], axis=1)
    mine = call(
        pack_kernel,
        ((MINE, B), BF),
        "pack",
        [
            (VMEM, jnp.pad(meta, ((0, 15), (0, B - K - 1)))),
            (HBM, d_out_t),
            (HBM, block_vals.reshape(K * B, B)),
        ],
        [pltpu.SemaphoreType.DMA((2,))],
    )
    with jax.named_scope("swap_core"):
        peer = lax.ppermute(mine, "c", [(0, 1), (1, 0)])
    with jax.named_scope("gather_x"):
        a = lax.all_to_all(jnp.broadcast_to(a, (NP, NZ, FL, B)), ("w", "x"), 0, 0, tiled=True)
    my_idx = meta[0]
    peer_idx = peer[META, : K + 1].astype(jnp.int32)
    parts = call(
        agg_kernel,
        ((NC, FL, B), F32),
        "agg",
        [(SMEM, my_idx), (SMEM, peer_idx), (VMEM, mine), (VMEM, peer), (VMEM, a)],
    )
    with jax.named_scope("pair_agg"):
        parts = lax.all_gather(parts, "c", axis=0, tiled=False)
    ride = call(
        ride_kernel,
        ((NY, RIDE, B), BF),
        "ride",
        [(VMEM, parts), (VMEM, mine), (VMEM, peer), (VMEM, weight)],
    )
    with jax.named_scope("share_agg"):
        ride = lax.all_to_all(ride, "y", 0, 0, tiled=True)
    out_t, term = call(
        back_kernel,
        [((HL, B), BF), ((NP, NZ * FL + FL, B), BF)],
        "back",
        [(HBM, my_idx), (HBM, peer_idx), (VMEM, ride), (VMEM, mine), (VMEM, peer)],
        [pltpu.VMEM((NP * NZ + 1, FL, B), F32), pltpu.VMEM((2, B, NC * B), BF)]
        + [pltpu.VMEM((2 * B, NC * B), BF)]
        + [pltpu.SMEM((K + 1,), jnp.int32)] * 2
        + [pltpu.SemaphoreType.DMA((3,))],
        (HBM, VMEM),
    )
    with jax.named_scope("scatter_x"):
        term = lax.all_to_all(term, ("w", "x"), 0, 0, tiled=True)
    term = call(sum_kernel, ((NZ, 2 * FL, B), BF), "sum_x", [(VMEM, term)])
    with jax.named_scope("scatter_z"):
        term = lax.all_to_all(term, "z", 0, 0, tiled=True)
    half = call(half_kernel, ((FL, B), F32), "half", [(VMEM, term)])
    with jax.named_scope("join_w"):
        halves = lax.all_gather(half, "c", axis=0, tiled=False)
    grad_w, grad_x = call(
        last_kernel,
        [((FL, 2 * B), F32), ((FL, B), F32)],
        "last",
        [(VMEM, term), (VMEM, halves)],
    )
    return (out_t, grad_w, grad_x)


def solution(mesh):
    fine = Mesh(mesh.devices.reshape(NZ, NW, NX, NC, NY), ("z", "w", "x", "c", "y"))
    nodes = ("z", "w", "x", "c")
    return jax.shard_map(
        local,
        mesh=fine,
        in_specs=(
            P("y", nodes),
            P("y", None),
            P(nodes, None),
            P(nodes),
            P(nodes, None, None, None),
            P("y", nodes),
        ),
        out_specs=(P("y", nodes), P("y", None), P("y", nodes)),
        check_vma=False,
    )
```
